512 devices in a mesh: seq: 8 (over z_lo, core), row: 4 (over y), col: 16 (over z_hi, x).
Axes of the slice: x: 4, y: 4, z: 16 (z_hi: 4, z_lo: 4; z = z_hi * 4 + z_lo), core: 2. Of those that a mesh axis runs over, the one named last changes fastest.
Arguments:
- stream: bfloat16 [2048, 4096], P('seq', ('row', 'col')), may hold values from -6 to 6
- query_heads: bfloat16 [2048, 4096], P('seq', ('row', 'col')), may hold values from -24 to 24
- key_heads: bfloat16 [2048, 4096], P('seq', ('row', 'col')), may hold values from -24 to 24
- value_heads: bfloat16 [2048, 4096], P('seq', ('row', 'col')), may hold values from -6 to 6
- windows: int32 [64], replicated, may hold values from 32 to 256, as said below
- norm_gain: float32 [4096], P(('row', 'col')), may hold values from 0.4 to 1.6
- up_weight: bfloat16 [4096, 16384], P('row', ('seq', 'col')), may hold values from -0.125 to 0.125
- down_weight: bfloat16 [16384, 4096], P(('seq', 'col'), 'row'), may hold values from -0.0625 to 0.0625
- up_rows: int32 [2048], replicated, may hold values from 0 to 31, as said below
- up_cols: int32 [2048], replicated, may hold values from 0 to 127, as said below
- down_rows: int32 [2048], replicated, may hold values from 0 to 127, as said below
- down_cols: int32 [2048], replicated, may hold values from 0 to 31, as said below
- cotangent: bfloat16 [2048, 4096], P('seq', ('row', 'col')), may hold values from -6 to 6
Outputs:
- grad_stream: bfloat16 [2048, 4096], P('seq', ('row', 'col'))
- grad_query: bfloat16 [2048, 4096], P('seq', ('row', 'col'))
- grad_key: bfloat16 [2048, 4096], P('seq', ('row', 'col'))
- grad_value: bfloat16 [2048, 4096], P('seq', ('row', 'col'))
- grad_gain: float32 [4096], P(('row', 'col'))
- grad_up: bfloat16 [4096, 16384], P('row', ('seq', 'col'))
- grad_down: bfloat16 [16384, 4096], P(('seq', 'col'), 'row')
The draws below stay inside these ranges and needn't reach their ends.
Inputs may be any that keep to these rules, and one draw needn't show every extreme that they name: Some head has windows[h] exactly 256. The pairs (up_rows[t], up_cols[t]) are distinct: half of all blocks. `up_cols`: see up_rows. The pairs (down_rows[t], down_cols[t]) are distinct: half of all blocks. `down_cols`: see down_rows.
All inputs are finite; a program needn't handle non-finite values.
Results may differ from the reference program's by a relative error of at most 0.034.
Values may be sent and summed in bfloat16 or wider, within the bound.
No kernel may reach another device: no remote copies, remote signals or barrier semaphores. Data moves between devices by JAX's collectives and lax.ppermute only.
A program may use at most 64 MiB of HBM per device.

```python
import jax
import jax.numpy as jnp
from jax import lax

HD = 64
BLK = 128
FF = 16384
TOK_DEV = 256
HEADS = 64
D = 4096
SEQ = 2048
N_SEQ = 8


def draw_query_heads(key, part):
    key = jax.random.fold_in(key, 1)
    values = jnp.clip(jax.random.normal(key, (SEQ, D)), -6.0, 6.0)
    return values.astype(jnp.bfloat16)


def draw_key_heads(key, part):
    key = jax.random.fold_in(key, 2)
    values = jnp.clip(jax.random.normal(key, (SEQ, D)), -6.0, 6.0)
    return values.astype(jnp.bfloat16)


def draw_windows(key, part):
    key = jax.random.fold_in(key, 5)
    keys_two = jax.random.split(key, 2)
    reaches = jax.random.randint(keys_two[0], (HEADS,), TOK_DEV // 8, TOK_DEV + 1)
    widest = jax.random.randint(keys_two[1], (), 0, HEADS)
    return jnp.where(jnp.arange(HEADS, dtype=jnp.int32) == widest, TOK_DEV, reaches).astype(jnp.int32)


def pattern_pairs(key, salt, row_count, col_count):
    key = jax.random.fold_in(key, salt)
    keys_three = jax.random.split(key, 3)
    cells = row_count * col_count
    base = jax.random.randint(keys_three[0], (cells,), 0, 1024)
    row_bias = jax.random.randint(keys_three[1], (row_count,), 0, 512)
    col_bias = jax.random.randint(keys_three[2], (col_count,), 0, 512)
    places = jnp.arange(cells, dtype=jnp.int32)
    ranking = (base + row_bias[places // col_count] + col_bias[places % col_count]) * cells + places
    chosen = lax.top_k(ranking, cells // 2)[1].astype(jnp.int32)
    return ((chosen // col_count).astype(jnp.int32), (chosen % col_count).astype(jnp.int32))


def draw_up_rows(key, part):
    return pattern_pairs(key, 21, D // BLK, FF // BLK)[0]


def draw_up_cols(key, part):
    return pattern_pairs(key, 21, D // BLK, FF // BLK)[1]


def draw_down_rows(key, part):
    return pattern_pairs(key, 22, FF // BLK, D // BLK)[0]


def draw_down_cols(key, part):
    return pattern_pairs(key, 22, FF // BLK, D // BLK)[1]


def levels(rng, extent, pieces, smallest, largest):
    level, own = 1.0, jax.random.fold_in(rng, 6)
    for position, blocks in pieces:
        steps = jnp.exp(jax.random.uniform(jax.random.fold_in(own, position), (blocks,), jnp.float32, smallest / len(pieces), largest / len(pieces)))
        level = level * jnp.repeat(steps, extent[position] // blocks).reshape([-1 if axis == position else 1 for axis in range(len(extent))])
    return level


def bell_draw(rng, extent, width, reach, cuts=(), held_as=jnp.bfloat16):
    loudness = levels(rng, extent, cuts, -0.22, 0.18) if cuts else 1.0
    values = jax.random.normal(rng, extent, jnp.float32) * width * loudness
    return jnp.minimum(jnp.maximum(values, -reach), reach).astype(held_as)


def setup_inputs(seed: int = 0) -> dict:
    streams_of = jax.random.split(jax.random.key(seed), 14)
    stream = bell_draw(streams_of[0], (SEQ, D), 1.0, 6.0, ((0, 8), (1, 64)))
    query_heads = draw_query_heads(jax.random.fold_in(streams_of[13], 71), 0)
    key_heads = draw_key_heads(jax.random.fold_in(streams_of[13], 71), 0)
    value_heads = bell_draw(streams_of[3], (SEQ, D), 1.0, 6.0, ((0, 8), (1, 64)))
    windows = draw_windows(jax.random.fold_in(streams_of[13], 71), 0)
    norm_gain = jnp.clip(1.0 + 0.12 * jax.random.normal(streams_of[5], (D,), jnp.float32), 0.4, 1.6)
    up_weight = bell_draw(streams_of[6], (D, FF), (D // 2) ** -0.5, 0.125, ((0, 4), (1, 128)))
    down_weight = bell_draw(streams_of[7], (FF, D), (FF // 2) ** -0.5, 0.0625, ((0, 128), (1, 4)))
    up_rows = draw_up_rows(jax.random.fold_in(streams_of[13], 71), 0)
    up_cols = draw_up_cols(jax.random.fold_in(streams_of[13], 71), 0)
    down_rows = draw_down_rows(jax.random.fold_in(streams_of[13], 71), 0)
    down_cols = draw_down_cols(jax.random.fold_in(streams_of[13], 71), 0)
    cotangent = bell_draw(streams_of[12], (SEQ, D), 1.0, 6.0, ((0, 8), (1, 64)))
    return {"stream": stream, "query_heads": query_heads, "key_heads": key_heads, "value_heads": value_heads, "windows": windows, "norm_gain": norm_gain, "up_weight": up_weight, "down_weight": down_weight, "up_rows": up_rows, "up_cols": up_cols, "down_rows": down_rows, "down_cols": down_cols, "cotangent": cotangent}


GELU_C = 0.7978845608028654
GELU_A = 0.044715
EPSILON = 1e-05

def gelu_value(pre_act):
    tanh_arg = GELU_C * (pre_act + GELU_A * pre_act * pre_act * pre_act)
    return 0.5 * pre_act * (1.0 + jnp.tanh(tanh_arg))

def gelu_slope(pre_act):
    tanh_arg = GELU_C * (pre_act + GELU_A * pre_act * pre_act * pre_act)
    tanh_val = jnp.tanh(tanh_arg)
    return 0.5 * (1.0 + tanh_val) + 0.5 * pre_act * (1.0 - tanh_val * tanh_val) * GELU_C * (1.0 + 3.0 * GELU_A * pre_act * pre_act)

def block_mask(row_ids, col_ids, row_count, col_count):
    row_hot = (row_ids[:, None] == jnp.arange(row_count, dtype=jnp.int32)[None, :]).astype(jnp.float32)
    col_hot = (col_ids[:, None] == jnp.arange(col_count, dtype=jnp.int32)[None, :]).astype(jnp.float32)
    return jnp.dot(row_hot.T, col_hot, precision=lax.Precision.HIGHEST)

def apply_mask(weight, block_flags):
    row_len, col_len = weight.shape
    blocked = weight.reshape(row_len // BLK, BLK, col_len // BLK, BLK)
    return (blocked * block_flags.astype(weight.dtype)[:, None, :, None]).reshape(row_len, col_len)

def head_probs(query_rows, key_rows, reach_width, score_scale):
    places = jnp.arange(query_rows.shape[0], dtype=jnp.int32)
    reached = jnp.abs(places[:, None] - places[None, :]) <= reach_width
    scores = jnp.dot(query_rows, key_rows.T, preferred_element_type=jnp.float32) * score_scale
    scores = jnp.where(reached, scores, -1e+30)
    row_peak = lax.optimization_barrier(jnp.max(scores, axis=1, keepdims=True))
    weights = jnp.where(reached, jnp.exp(scores - row_peak), 0.0)
    return weights / lax.optimization_barrier(jnp.sum(weights, axis=1, keepdims=True))

def block_sum(left_side, right_side):

    def add_block(running, block_index):
        first_row = block_index * TOK_DEV
        left_rows = lax.dynamic_slice_in_dim(left_side, first_row, TOK_DEV, 0)
        right_rows = lax.dynamic_slice_in_dim(right_side, first_row, TOK_DEV, 0)
        block_term = jnp.dot(left_rows.T, right_rows, preferred_element_type=jnp.float32).astype(jnp.bfloat16)
        block_term = lax.optimization_barrier(block_term)
        return (running + block_term.astype(jnp.float32), None)
    zero_sum = jnp.zeros((left_side.shape[1], right_side.shape[1]), jnp.float32)
    running, unused = lax.scan(add_block, zero_sum, jnp.arange(N_SEQ, dtype=jnp.int32))
    return running

def reference(stream, query_heads, key_heads, value_heads, windows, norm_gain, up_weight, down_weight, up_rows, up_cols, down_rows, down_cols, cotangent):
    score_scale = float(HD) ** (-0.5)

    def to_heads(array):
        return array.reshape(SEQ, HEADS, HD).transpose(1, 0, 2)

    def from_heads(array):
        return array.transpose(1, 0, 2).reshape(SEQ, D)

    def forward_head(packed):
        query_rows, key_rows, value_rows, reach_width = packed
        probs = head_probs(query_rows, key_rows, reach_width, score_scale)
        return jnp.dot(probs.astype(jnp.bfloat16), value_rows, preferred_element_type=jnp.float32)
    attended = from_heads(lax.map(forward_head, (to_heads(query_heads), to_heads(key_heads), to_heads(value_heads), windows)))
    hidden = (stream.astype(jnp.float32) + attended).astype(jnp.bfloat16)
    hidden_f = hidden.astype(jnp.float32)
    inv_rms = lax.rsqrt(lax.optimization_barrier(jnp.mean(hidden_f * hidden_f, axis=1, keepdims=True)) + EPSILON)
    normed = (hidden_f * inv_rms * norm_gain).astype(jnp.bfloat16)
    up_flags = block_mask(up_rows, up_cols, D // BLK, FF // BLK)
    down_flags = block_mask(down_rows, down_cols, FF // BLK, D // BLK)
    up_masked = apply_mask(up_weight, up_flags)
    down_masked = apply_mask(down_weight, down_flags)
    pre_act = jnp.dot(normed, up_masked, preferred_element_type=jnp.float32)
    activation = gelu_value(pre_act).astype(jnp.bfloat16)
    grad_pre = jnp.dot(cotangent, down_masked.T, preferred_element_type=jnp.float32)
    grad_act = (grad_pre * gelu_slope(pre_act)).astype(jnp.bfloat16)
    grad_down = apply_mask(block_sum(activation, cotangent), down_flags).astype(jnp.bfloat16)
    grad_up = apply_mask(block_sum(normed, grad_act), up_flags).astype(jnp.bfloat16)
    grad_norm = jnp.dot(grad_act, up_masked.T, preferred_element_type=jnp.float32)
    grad_gain = lax.optimization_barrier(jnp.sum(grad_norm * hidden_f * inv_rms, axis=0))
    gained = grad_norm * norm_gain
    token_total = lax.optimization_barrier(jnp.sum(gained * hidden_f, axis=1, keepdims=True))
    grad_hidden = inv_rms * gained - hidden_f * inv_rms * inv_rms * inv_rms * token_total / D + cotangent.astype(jnp.float32)
    grad_stream = grad_hidden.astype(jnp.bfloat16)

    def backward_head(packed):
        query_rows, key_rows, value_rows, reach_width, upstream = packed
        probs = head_probs(query_rows, key_rows, reach_width, score_scale)
        probs_low = probs.astype(jnp.bfloat16)
        grad_probs = jnp.dot(upstream, value_rows.T, preferred_element_type=jnp.float32)
        center = lax.optimization_barrier(jnp.sum(probs * grad_probs, axis=1, keepdims=True))
        grad_scores = (probs * (grad_probs - center)).astype(jnp.bfloat16)
        query_grad = jnp.dot(grad_scores, key_rows, preferred_element_type=jnp.float32) * score_scale
        key_grad = jnp.dot(grad_scores.T, query_rows, preferred_element_type=jnp.float32) * score_scale
        value_grad = jnp.dot(probs_low.T, upstream, preferred_element_type=jnp.float32)
        return (query_grad.astype(jnp.bfloat16), key_grad.astype(jnp.bfloat16), value_grad.astype(jnp.bfloat16))
    query_grad, key_grad, value_grad = lax.map(backward_head, (to_heads(query_heads), to_heads(key_heads), to_heads(value_heads), windows, to_heads(grad_stream)))
    return (grad_stream, from_heads(query_grad), from_heads(key_grad), from_heads(value_grad), grad_gain, grad_up, grad_down)
```

```python
import jax
import jax.numpy as jnp
from jax import lax
from jax.sharding import Mesh
from jax.sharding import PartitionSpec as P

BLK = 128
GELU_C = 0.7978845608028654
GELU_A = 0.044715
EPSILON = 1e-05
TAIL = 16
BF = jnp.bfloat16
F32 = jnp.float32


def gelu_value(pre_act):
    tanh_arg = GELU_C * (pre_act + GELU_A * pre_act * pre_act * pre_act)
    return 0.5 * pre_act * (1.0 + jnp.tanh(tanh_arg))


def gelu_slope(pre_act):
    tanh_arg = GELU_C * (pre_act + GELU_A * pre_act * pre_act * pre_act)
    tanh_val = jnp.tanh(tanh_arg)
    return 0.5 * (1.0 + tanh_val) + 0.5 * pre_act * (1.0 - tanh_val * tanh_val) * GELU_C * (
        1.0 + 3.0 * GELU_A * pre_act * pre_act
    )


def tail_rows(vector):
    high = lax.reduce_precision(vector, 8, 7)
    low = vector - high
    pair = jnp.stack([high, low]).astype(BF)
    return jnp.pad(pair, ((0, TAIL - 2), (0, 0)))


def tail_value(rows):
    return rows[..., 0, :].astype(F32) + rows[..., 1, :].astype(F32)


def spread(array, axis):
    count = lax.axis_size(axis)
    copies = jnp.broadcast_to(array[None], (count,) + array.shape)
    return lax.all_to_all(copies, axis, 0, 0, tiled=True)


def exchange(pieces, axis):
    return lax.all_to_all(pieces, axis, 0, 0, tiled=True)


def own_flags(inner_ids, outer_ids, own_outer, first_inner, inner_count):
    wanted = first_inner + jnp.arange(inner_count, dtype=jnp.int32)
    hit = (inner_ids[None, :] == wanted[:, None]) & (outer_ids == own_outer)[None, :]
    return jnp.any(hit, axis=1)


def on_device(
    stream,
    query_heads,
    key_heads,
    value_heads,
    windows,
    norm_gain,
    up_weight,
    down_weight,
    up_rows,
    up_cols,
    down_rows,
    down_cols,
    cotangent,
):
    tok, head = stream.shape
    n_zl, n_core, n_row, n_zh, n_x = (lax.axis_size(a) for a in ("zl", "core", "row", "zh", "x"))
    seq_devs = n_zl * n_core
    col_devs = n_zh * n_x
    seq_index = lax.axis_index(("zl", "core"))
    row_index = lax.axis_index("row")
    col_index = lax.axis_index(("zh", "x"))
    width_total = head * n_row * col_devs
    depth, units = up_weight.shape
    blocks = depth // BLK
    score_scale = float(head) ** (-0.5)
    swap = [(i, n_core - 1 - i) for i in range(n_core)]

    own_block = seq_index * col_devs + col_index
    up_flags = own_flags(up_rows, up_cols, own_block, row_index * blocks, blocks)
    down_flags = own_flags(down_cols, down_rows, own_block, row_index * blocks, blocks)
    up_own = up_weight.reshape(blocks, BLK, units) * up_flags.astype(BF)[:, None, None]
    down_own = down_weight.reshape(units, blocks, BLK).transpose(1, 0, 2)
    down_own = down_own * down_flags.astype(BF)[:, None, None]
    both = jnp.concatenate([up_own, down_own], axis=0)
    both = lax.all_gather(both, "zl", axis=0, tiled=False)
    up_all = both[:, :blocks].reshape(n_zl, depth, units)
    down_all = both[:, blocks:]

    query_t, stream_t, cot_t = query_heads.T, stream.T, cotangent.T
    paired = jnp.concatenate([key_heads.T, value_heads.T], axis=0)
    up_pairs = [(i, i + 1) for i in range(seq_devs - 1)]
    before = lax.ppermute(paired, ("zl", "core"), up_pairs)
    after = lax.ppermute(paired, ("zl", "core"), [(j, i) for i, j in up_pairs])
    widened = jnp.concatenate([before, paired, after], axis=1)
    key_ext, value_ext = widened[:head], widened[head:]
    reach_width = lax.dynamic_index_in_dim(
        windows, row_index * col_devs + col_index, 0, keepdims=False
    )
    query_place = seq_index * tok + jnp.arange(tok, dtype=jnp.int32)
    key_place = (seq_index - 1) * tok + jnp.arange(3 * tok, dtype=jnp.int32)
    reached = (
        (jnp.abs(query_place[None, :] - key_place[:, None]) <= reach_width)
        & (key_place[:, None] >= 0)
        & (key_place[:, None] < tok * seq_devs)
    )
    scores = jnp.dot(key_ext.T, query_t, preferred_element_type=F32) * score_scale
    scores = jnp.where(reached, scores, -1e30)
    peak = jnp.max(scores, axis=0, keepdims=True)
    weights = jnp.where(reached, jnp.exp(scores - peak), 0.0)
    probs = weights / jnp.sum(weights, axis=0, keepdims=True)
    probs_low = probs.astype(BF)
    attended = jnp.dot(value_ext, probs_low, preferred_element_type=F32)
    hidden = (stream_t.astype(F32) + attended).astype(BF)
    hidden_f = hidden.astype(F32)
    gain = norm_gain[:, None]
    gained = (hidden_f * gain).astype(BF)
    squares = jnp.sum(hidden_f * hidden_f, axis=0)

    send = jnp.concatenate([gained, cot_t, tail_rows(squares)], axis=0)
    panel = lax.all_gather(send, "zh", axis=0, tiled=False)
    panel = spread(panel, "x")
    other = lax.ppermute(panel, "core", swap)
    panel = jnp.concatenate([panel, other], axis=3).transpose(1, 0, 2, 3)
    feats = panel[:, :, :head].reshape(depth, n_core * tok)
    cots = panel[:, :, head : 2 * head].reshape(depth, n_core * tok)
    square_part = jnp.sum(tail_value(panel[:, :, 2 * head :]), axis=(0, 1))

    pre_part = jnp.einsum("zdf,dt->zft", up_all, feats, preferred_element_type=F32)
    cot_blocks = cots.reshape(blocks, BLK, n_core * tok)
    grad_part = jnp.einsum("zbfd,bdt->zft", down_all, cot_blocks, preferred_element_type=F32)
    square_tail = jnp.broadcast_to(tail_rows(square_part)[None], (n_zl, TAIL, n_core * tok))
    parts = jnp.concatenate([pre_part.astype(BF), grad_part.astype(BF), square_tail], axis=1)
    parts = exchange(parts, "row")
    summed = jnp.sum(parts[:, : 2 * units].astype(F32), axis=0)
    square_total = jnp.sum(tail_value(parts[:, 2 * units :]), axis=0)
    inv_rms = lax.rsqrt(square_total / width_total + EPSILON)
    pre_act = summed[:units] * inv_rms
    activation = gelu_value(pre_act).astype(BF)
    grad_act = (summed[units:] * gelu_slope(pre_act) * inv_rms).astype(BF)
    inner_part = jnp.sum(grad_act.astype(F32) * pre_act, axis=0)
    acts = spread(jnp.concatenate([activation, grad_act, tail_rows(inner_part)], axis=0), "row")
    act_all, grad_all = acts[:, :units], acts[:, units : 2 * units]
    inner_part = jnp.sum(tail_value(acts[:, 2 * units :]), axis=0)

    norm_part = jnp.einsum("zdf,zft->dt", up_all, grad_all, preferred_element_type=F32).astype(BF)
    norm_part = jnp.concatenate([norm_part, tail_rows(inner_part)], axis=0)
    theirs = lax.ppermute(norm_part[:, tok:], "core", swap)
    norm_sum = (norm_part[:depth, :tok].astype(F32) + theirs[:depth].astype(F32)).astype(BF)
    inner_part = tail_value(norm_part[depth:, :tok]) + tail_value(theirs[depth:])
    pieces = norm_sum.reshape(n_zh, n_x, head, tok).transpose(1, 0, 2, 3)
    pieces = pieces.reshape(n_x, n_zh * head, tok)
    inner_tail = jnp.broadcast_to(tail_rows(inner_part)[None], (n_x, TAIL, tok))
    pieces = exchange(jnp.concatenate([pieces, inner_tail], axis=1), "x")
    norm_sum = jnp.sum(pieces[:, : n_zh * head].astype(F32), axis=0).astype(BF)
    inner_part = jnp.sum(tail_value(pieces[:, n_zh * head :]), axis=0)
    inner_tail = jnp.broadcast_to(tail_rows(inner_part)[None], (n_zh, TAIL, tok))
    pieces = jnp.concatenate([norm_sum.reshape(n_zh, head, tok), inner_tail], axis=1)
    pieces = exchange(pieces, "zh")
    grad_norm = jnp.sum(pieces[:, :head].astype(F32), axis=0)
    inner = jnp.sum(tail_value(pieces[:, head:]), axis=0)

    grad_up_part = jnp.einsum("dt,zft->zdf", feats, grad_all, preferred_element_type=F32)
    grad_up_part = grad_up_part.astype(BF).reshape(n_zl, blocks, BLK, units)
    grad_down_part = jnp.einsum("zft,bdt->zbfd", act_all, cot_blocks, preferred_element_type=F32)
    grad_parts = jnp.concatenate([grad_up_part, grad_down_part.astype(BF)], axis=1)
    grad_parts = grad_parts.reshape(n_zl * 2 * depth, units)
    grads = lax.psum_scatter(grad_parts, "zl", scatter_dimension=0, tiled=True)
    grads = grads.reshape(2 * blocks, BLK, units)
    grad_up = grads[:blocks] * up_flags.astype(BF)[:, None, None]
    grad_up = grad_up.reshape(depth, units)
    grad_down = grads[blocks:] * down_flags.astype(BF)[:, None, None]
    grad_down = grad_down.transpose(1, 0, 2).reshape(units, depth)

    grad_gain = lax.psum(jnp.sum(grad_norm * hidden_f, axis=1), ("zl", "core"))
    scale = inv_rms[:tok] * inner / width_total
    grad_hidden = gain * grad_norm - hidden_f * scale + cot_t.astype(F32)
    grad_stream = grad_hidden.astype(BF)
    grad_probs = jnp.dot(value_ext.T, grad_stream, preferred_element_type=F32)
    center = jnp.sum(probs * grad_probs, axis=0, keepdims=True)
    grad_scores = (probs * (grad_probs - center)).astype(BF)
    grad_query = (jnp.dot(key_ext, grad_scores, preferred_element_type=F32) * score_scale).astype(BF)
    key_grad = jnp.dot(query_t, grad_scores.T, preferred_element_type=F32) * score_scale
    value_grad = jnp.dot(grad_stream, probs_low.T, preferred_element_type=F32)
    pair_grads = jnp.concatenate([key_grad, value_grad], axis=0)
    from_upper = lax.ppermute(
        pair_grads[:, :tok].astype(BF), ("zl", "core"), [(j, i) for i, j in up_pairs]
    )
    from_lower = lax.ppermute(pair_grads[:, 2 * tok :].astype(BF), ("zl", "core"), up_pairs)
    pair_total = pair_grads[:, tok : 2 * tok] + from_upper.astype(F32) + from_lower.astype(F32)
    pair_total = pair_total.astype(BF)
    return (
        grad_stream.T,
        grad_query.T,
        pair_total[:head].T,
        pair_total[head:].T,
        grad_gain,
        grad_up,
        grad_down,
    )


def solution(mesh):
    seq, row, col = (mesh.shape[a] for a in ("seq", "row", "col"))
    fine = Mesh(
        mesh.devices.reshape(seq // 2, 2, row, 4, col // 4), ("zl", "core", "row", "zh", "x")
    )
    features = P(("zl", "core"), ("row", "zh", "x"))
    gain_spec = P(("row", "zh", "x"))
    up_spec = P("row", ("zl", "core", "zh", "x"))
    down_spec = P(("zl", "core", "zh", "x"), "row")
    in_specs = (
        (features,) * 4 + (P(), gain_spec, up_spec, down_spec) + (P(),) * 4 + (features,)
    )
    out_specs = (features,) * 4 + (gain_spec, up_spec, down_spec)
    return jax.shard_map(
        on_device, mesh=fine, in_specs=in_specs, out_specs=out_specs, check_vma=False
    )
```

```python
import jax
import jax.numpy as jnp
from jax import lax
from jax.sharding import Mesh
from jax.sharding import PartitionSpec as P

BLK = 128
GELU_C = 0.7978845608028654
GELU_A = 0.044715
EPSILON = 1e-05
TAIL = 16
BF = jnp.bfloat16
F32 = jnp.float32


def gelu_value(pre_act):
    tanh_arg = GELU_C * (pre_act + GELU_A * pre_act * pre_act * pre_act)
    return 0.5 * pre_act * (1.0 + jnp.tanh(tanh_arg))


def gelu_slope(pre_act):
    tanh_arg = GELU_C * (pre_act + GELU_A * pre_act * pre_act * pre_act)
    tanh_val = jnp.tanh(tanh_arg)
    return 0.5 * (1.0 + tanh_val) + 0.5 * pre_act * (1.0 - tanh_val * tanh_val) * GELU_C * (
        1.0 + 3.0 * GELU_A * pre_act * pre_act
    )


def tail_rows(vector):
    high = lax.reduce_precision(vector, 8, 7)
    low = vector - high
    pair = jnp.stack([high, low]).astype(BF)
    return jnp.pad(pair, ((0, TAIL - 2), (0, 0)))


def tail_value(rows):
    return rows[..., 0, :].astype(F32) + rows[..., 1, :].astype(F32)


def spread(array, axis):
    count = lax.axis_size(axis)
    copies = jnp.broadcast_to(array[None], (count,) + array.shape)
    return lax.all_to_all(copies, axis, 0, 0, tiled=True)


def exchange(pieces, axis):
    return lax.all_to_all(pieces, axis, 0, 0, tiled=True)


def own_flags(inner_ids, outer_ids, own_outer, first_inner, inner_count):
    wanted = first_inner + jnp.arange(inner_count, dtype=jnp.int32)
    hit = (inner_ids[None, :] == wanted[:, None]) & (outer_ids == own_outer)[None, :]
    return jnp.any(hit, axis=1)


def window_send(array, slot, n_zh, n_zl, n_core, home):
    ring = n_zh * n_zl
    pairs = []
    for place in range(ring):
        for core in range(n_core):
            step = (slot - n_zl // 2) * (1 if core == 0 else -1)
            owner, worker = (
                ((z % n_zl) * n_core + core) * n_zh + z // n_zl for z in ((place + step) % ring, place)
            )
            pairs.append((worker, owner) if home else (owner, worker))
    if all(source == target for source, target in pairs):
        return array
    return lax.ppermute(array, ("zl", "core", "zh"), pairs)


def on_device(
    stream,
    query_heads,
    key_heads,
    value_heads,
    windows,
    norm_gain,
    up_weight,
    down_weight,
    up_rows,
    up_cols,
    down_rows,
    down_cols,
    cotangent,
):
    tok, head = stream.shape
    n_zl, n_core, n_row, n_zh, n_x = (lax.axis_size(a) for a in ("zl", "core", "row", "zh", "x"))
    seq_devs = n_zl * n_core
    col_devs = n_zh * n_x
    seq_index = lax.axis_index(("zl", "core"))
    row_index = lax.axis_index("row")
    col_index = lax.axis_index(("zh", "x"))
    width_total = head * n_row * col_devs
    depth, units = up_weight.shape
    blocks = depth // BLK
    score_scale = float(head) ** (-0.5)
    swap = [(i, n_core - 1 - i) for i in range(n_core)]

    own_block = seq_index * col_devs + col_index
    up_flags = own_flags(up_rows, up_cols, own_block, row_index * blocks, blocks)
    down_flags = own_flags(down_cols, down_rows, own_block, row_index * blocks, blocks)
    up_own = up_weight.reshape(blocks, BLK, units) * up_flags.astype(BF)[:, None, None]
    down_own = down_weight.reshape(units, blocks, BLK).transpose(1, 0, 2)
    down_own = down_own * down_flags.astype(BF)[:, None, None]
    both = jnp.concatenate([up_own, down_own], axis=0)
    slots = [window_send(both, w, n_zh, n_zl, n_core, False) for w in range(n_zl)]
    up_all = jnp.stack([slot[:blocks] for slot in slots]).reshape(n_zl, depth, units)
    down_all = jnp.stack([slot[blocks:] for slot in slots])

    query_t, stream_t, cot_t = query_heads.T, stream.T, cotangent.T
    paired = jnp.concatenate([key_heads.T, value_heads.T], axis=0)
    up_pairs = [(i, i + 1) for i in range(seq_devs - 1)]
    before = lax.ppermute(paired, ("zl", "core"), up_pairs)
    after = lax.ppermute(paired, ("zl", "core"), [(j, i) for i, j in up_pairs])
    widened = jnp.concatenate([before, paired, after], axis=1)
    key_ext, value_ext = widened[:head], widened[head:]
    reach_width = lax.dynamic_index_in_dim(
        windows, row_index * col_devs + col_index, 0, keepdims=False
    )
    query_place = seq_index * tok + jnp.arange(tok, dtype=jnp.int32)
    key_place = (seq_index - 1) * tok + jnp.arange(3 * tok, dtype=jnp.int32)
    reached = (
        (jnp.abs(query_place[None, :] - key_place[:, None]) <= reach_width)
        & (key_place[:, None] >= 0)
        & (key_place[:, None] < tok * seq_devs)
    )
    scores = jnp.dot(key_ext.T, query_t, preferred_element_type=F32) * score_scale
    scores = jnp.where(reached, scores, -1e30)
    peak = jnp.max(scores, axis=0, keepdims=True)
    weights = jnp.where(reached, jnp.exp(scores - peak), 0.0)
    probs = weights / jnp.sum(weights, axis=0, keepdims=True)
    probs_low = probs.astype(BF)
    attended = jnp.dot(value_ext, probs_low, preferred_element_type=F32)
    hidden = (stream_t.astype(F32) + attended).astype(BF)
    hidden_f = hidden.astype(F32)
    gain = norm_gain[:, None]
    gained = (hidden_f * gain).astype(BF)
    squares = jnp.sum(hidden_f * hidden_f, axis=0)

    send = jnp.concatenate([gained, cot_t, tail_rows(squares)], axis=0)
    panel = lax.all_gather(send, "zh", axis=0, tiled=False)
    panel = spread(panel, "x")
    other = lax.ppermute(panel, "core", swap)
    panel = jnp.concatenate([panel, other], axis=3).transpose(1, 0, 2, 3)
    feats = panel[:, :, :head].reshape(depth, n_core * tok)
    cots = panel[:, :, head : 2 * head].reshape(depth, n_core * tok)
    square_part = jnp.sum(tail_value(panel[:, :, 2 * head :]), axis=(0, 1))

    pre_part = jnp.einsum("zdf,dt->zft", up_all, feats, preferred_element_type=F32)
    cot_blocks = cots.reshape(blocks, BLK, n_core * tok)
    grad_part = jnp.einsum("zbfd,bdt->zft", down_all, cot_blocks, preferred_element_type=F32)
    square_tail = jnp.broadcast_to(tail_rows(square_part)[None], (n_zl, TAIL, n_core * tok))
    parts = jnp.concatenate([pre_part.astype(BF), grad_part.astype(BF), square_tail], axis=1)
    parts = exchange(parts, "row")
    summed = jnp.sum(parts[:, : 2 * units].astype(F32), axis=0)
    square_total = jnp.sum(tail_value(parts[:, 2 * units :]), axis=0)
    inv_rms = lax.rsqrt(square_total / width_total + EPSILON)
    pre_act = summed[:units] * inv_rms
    activation = gelu_value(pre_act).astype(BF)
    grad_act = (summed[units:] * gelu_slope(pre_act) * inv_rms).astype(BF)
    inner_part = jnp.sum(grad_act.astype(F32) * pre_act, axis=0)
    acts = spread(jnp.concatenate([activation, grad_act, tail_rows(inner_part)], axis=0), "row")
    act_all, grad_all = acts[:, :units], acts[:, units : 2 * units]
    inner_part = jnp.sum(tail_value(acts[:, 2 * units :]), axis=0)

    norm_part = jnp.einsum("zdf,zft->dt", up_all, grad_all, preferred_element_type=F32).astype(BF)
    norm_part = jnp.concatenate([norm_part, tail_rows(inner_part)], axis=0)
    theirs = lax.ppermute(norm_part[:, tok:], "core", swap)
    norm_sum = (norm_part[:depth, :tok].astype(F32) + theirs[:depth].astype(F32)).astype(BF)
    inner_part = tail_value(norm_part[depth:, :tok]) + tail_value(theirs[depth:])
    pieces = norm_sum.reshape(n_zh, n_x, head, tok).transpose(1, 0, 2, 3)
    pieces = pieces.reshape(n_x, n_zh * head, tok)
    inner_tail = jnp.broadcast_to(tail_rows(inner_part)[None], (n_x, TAIL, tok))
    pieces = exchange(jnp.concatenate([pieces, inner_tail], axis=1), "x")
    norm_sum = jnp.sum(pieces[:, : n_zh * head].astype(F32), axis=0).astype(BF)
    inner_part = jnp.sum(tail_value(pieces[:, n_zh * head :]), axis=0)
    inner_tail = jnp.broadcast_to(tail_rows(inner_part)[None], (n_zh, TAIL, tok))
    pieces = jnp.concatenate([norm_sum.reshape(n_zh, head, tok), inner_tail], axis=1)
    pieces = exchange(pieces, "zh")
    grad_norm = jnp.sum(pieces[:, :head].astype(F32), axis=0)
    inner = jnp.sum(tail_value(pieces[:, head:]), axis=0)

    grad_up_part = jnp.einsum("dt,zft->zdf", feats, grad_all, preferred_element_type=F32)
    grad_up_part = grad_up_part.astype(BF).reshape(n_zl, blocks, BLK, units)
    grad_down_part = jnp.einsum("zft,bdt->zbfd", act_all, cot_blocks, preferred_element_type=F32)
    grad_parts = jnp.concatenate([grad_up_part, grad_down_part.astype(BF)], axis=1)
    grads = sum(
        window_send(grad_parts[w], w, n_zh, n_zl, n_core, True).astype(F32) for w in range(n_zl)
    )
    grad_up = (grads[:blocks] * up_flags.astype(F32)[:, None, None]).astype(BF)
    grad_up = grad_up.reshape(depth, units)
    grad_down = (grads[blocks:] * down_flags.astype(F32)[:, None, None]).astype(BF)
    grad_down = grad_down.transpose(1, 0, 2).reshape(units, depth)

    grad_gain = lax.psum(jnp.sum(grad_norm * hidden_f, axis=1), ("zl", "core"))
    scale = inv_rms[:tok] * inner / width_total
    grad_hidden = gain * grad_norm - hidden_f * scale + cot_t.astype(F32)
    grad_stream = grad_hidden.astype(BF)
    grad_probs = jnp.dot(value_ext.T, grad_stream, preferred_element_type=F32)
    center = jnp.sum(probs * grad_probs, axis=0, keepdims=True)
    grad_scores = (probs * (grad_probs - center)).astype(BF)
    grad_query = (jnp.dot(key_ext, grad_scores, preferred_element_type=F32) * score_scale).astype(BF)
    key_grad = jnp.dot(query_t, grad_scores.T, preferred_element_type=F32) * score_scale
    value_grad = jnp.dot(grad_stream, probs_low.T, preferred_element_type=F32)
    pair_grads = jnp.concatenate([key_grad, value_grad], axis=0)
    from_upper = lax.ppermute(
        pair_grads[:, :tok].astype(BF), ("zl", "core"), [(j, i) for i, j in up_pairs]
    )
    from_lower = lax.ppermute(pair_grads[:, 2 * tok :].astype(BF), ("zl", "core"), up_pairs)
    pair_total = pair_grads[:, tok : 2 * tok] + from_upper.astype(F32) + from_lower.astype(F32)
    pair_total = pair_total.astype(BF)
    return (
        grad_stream.T,
        grad_query.T,
        pair_total[:head].T,
        pair_total[head:].T,
        grad_gain,
        grad_up,
        grad_down,
    )


def solution(mesh):
    seq, row, col = (mesh.shape[a] for a in ("seq", "row", "col"))
    fine = Mesh(
        mesh.devices.reshape(seq // 2, 2, row, 4, col // 4), ("zl", "core", "row", "zh", "x")
    )
    features = P(("zl", "core"), ("row", "zh", "x"))
    gain_spec = P(("row", "zh", "x"))
    up_spec = P("row", ("zl", "core", "zh", "x"))
    down_spec = P(("zl", "core", "zh", "x"), "row")
    in_specs = (
        (features,) * 4 + (P(), gain_spec, up_spec, down_spec) + (P(),) * 4 + (features,)
    )
    out_specs = (features,) * 4 + (gain_spec, up_spec, down_spec)
    return jax.shard_map(
        on_device, mesh=fine, in_specs=in_specs, out_specs=out_specs, check_vma=False
    )
```

```python
import functools

import jax
import jax.numpy as jnp
from jax import lax
from jax.experimental import pallas as pl
from jax.experimental.pallas import tpu as pltpu
from jax.sharding import Mesh
from jax.sharding import PartitionSpec as P

BLK = 128
GELU_C = 0.7978845608028654
GELU_A = 0.044715
EPSILON = 1e-05
TAIL = 16
BF = jnp.bfloat16
F32 = jnp.float32


def gelu_value(pre_act):
    tanh_arg = GELU_C * (pre_act + GELU_A * pre_act * pre_act * pre_act)
    return 0.5 * pre_act * (1.0 + jnp.tanh(tanh_arg))


def gelu_slope(pre_act):
    tanh_arg = GELU_C * (pre_act + GELU_A * pre_act * pre_act * pre_act)
    tanh_val = jnp.tanh(tanh_arg)
    return 0.5 * (1.0 + tanh_val) + 0.5 * pre_act * (1.0 - tanh_val * tanh_val) * GELU_C * (
        1.0 + 3.0 * GELU_A * pre_act * pre_act
    )


def tail_rows(vector):
    high = lax.reduce_precision(vector, 8, 7)
    low = vector - high
    pair = jnp.stack([high, low]).astype(BF)
    return jnp.pad(pair, ((0, TAIL - 2), (0, 0)))


def tail_value(rows):
    return rows[..., 0, :].astype(F32) + rows[..., 1, :].astype(F32)


def spread(array, axis):
    count = lax.axis_size(axis)
    copies = jnp.broadcast_to(array[None], (count,) + array.shape)
    return lax.all_to_all(copies, axis, 0, 0, tiled=True)


def exchange(pieces, axis):
    return lax.all_to_all(pieces, axis, 0, 0, tiled=True)


def window_send(array, slot, n_zh, n_zl, n_core, home):
    ring = n_zh * n_zl
    pairs = []
    for place in range(ring):
        for core in range(n_core):
            step = (slot - n_zl // 2) * (1 if core == 0 else -1)
            owner, worker = (
                ((z % n_zl) * n_core + core) * n_zh + z // n_zl for z in ((place + step) % ring, place)
            )
            pairs.append((worker, owner) if home else (owner, worker))
    if all(source == target for source, target in pairs):
        return array
    return lax.ppermute(array, ("zl", "core", "zh"), pairs)


def call_kernel(body, out_shapes, flops, *operands, loads=0, scratch=()):
    moved = sum(a.size * a.dtype.itemsize for a in operands)
    moved += sum(a.size * a.dtype.itemsize for a in out_shapes)
    vmem = pl.BlockSpec(memory_space=pltpu.VMEM)
    smem = pl.BlockSpec(memory_space=pltpu.SMEM)
    return pl.pallas_call(
        body,
        out_shape=out_shapes,
        in_specs=[pl.BlockSpec(memory_space=pltpu.HBM)] * loads
        + [smem if a.ndim == 1 else vmem for a in operands[loads:]],
        out_specs=[vmem] * len(out_shapes),
        scratch_shapes=list(scratch) + ([pltpu.SemaphoreType.DMA((loads,))] if loads else []),
        compiler_params=pltpu.CompilerParams(vmem_limit_bytes=(60 if loads else 40) * 1024 * 1024),
        cost_estimate=pl.CostEstimate(flops=flops, bytes_accessed=moved, transcendentals=0),
    )(*operands)


def load_all(sources, targets, arrived):
    copies = [
        pltpu.make_async_copy(source, target, arrived.at[i])
        for i, (source, target) in enumerate(zip(sources, targets, strict=True))
    ]
    for copy in copies:
        copy.start()
    for copy in copies:
        copy.wait()


def held(array):
    return pltpu.VMEM(array.shape, array.dtype)


def shaped(shape, dtype):
    return jax.ShapeDtypeStruct(shape, dtype)


def dot_first(left, right):
    return lax.dot_general(left, right, (((0,), (0,)), ((), ())), preferred_element_type=F32)


def dot_last(left, right):
    return lax.dot_general(left, right, (((1,), (1,)), ((), ())), preferred_element_type=F32)


def dot_plain(left, right):
    return jnp.dot(left, right, preferred_element_type=F32)


def write_tail(ref, index, first, vector):
    high = vector.astype(BF)
    low = (vector - high.astype(F32)).astype(BF)
    place = lax.broadcasted_iota(jnp.int32, (TAIL, vector.shape[1]), 0)
    rows = jnp.where(place == 0, high.astype(F32), jnp.where(place == 1, low.astype(F32), 0.0))
    ref[index + (slice(first, first + TAIL), slice(None))] = rows.astype(BF)


def read_tail(rows):
    rows = rows.astype(F32)
    return rows[0:1] + rows[1:2]


def prepare_body(blocks, *refs):
    sources, (both_ref, flag_ref, pair_ref) = refs[:8], refs[8:11]
    up_ref, down_ref, up_in, up_out, down_in, down_out, arrived = refs[11:]
    head = sources[6].shape[0]
    pair_halves = (pair_ref.at[:head, :], pair_ref.at[head:, :])
    load_all(sources, (up_ref, down_ref, up_in, up_out, down_in, down_out) + pair_halves, arrived)
    col_devs = lax.axis_size("zh") * lax.axis_size("x")
    seq_index = lax.axis_index("zl") * lax.axis_size("core") + lax.axis_index("core")
    col_index = lax.axis_index("zh") * lax.axis_size("x") + lax.axis_index("x")
    own_block = seq_index * col_devs + col_index
    first = lax.axis_index("row") * blocks
    for kind, (inner, outer) in enumerate(((up_in, up_out), (down_in, down_out))):
        shifted = jnp.where(outer[...] == own_block, inner[...] - first, -1)
        for b in range(blocks):
            hit = jnp.where(shifted == b, 1.0, 0.0)
            flag = jnp.max(jnp.max(hit, axis=0, keepdims=True), axis=1, keepdims=True)
            flag_ref[kind * blocks + b : kind * blocks + b + 1, :] = jnp.broadcast_to(flag, (1, BLK))
            if kind == 0:
                block = up_ref[b * BLK : (b + 1) * BLK, :]
            else:
                block = down_ref[:, b * BLK : (b + 1) * BLK]
            both_ref[kind * blocks + b] = (block.astype(F32) * flag).astype(BF)


def column(row):
    count = row.shape[1]
    across = lax.broadcasted_iota(jnp.int32, (count, count), 1)
    down = lax.broadcasted_iota(jnp.int32, (count, count), 0)
    return jnp.sum(jnp.where(across == down, row, 0.0), axis=1, keepdims=True)


def reached_part(part, tok, seq_devs, reach):
    seq_index = lax.axis_index("zl") * lax.axis_size("core") + lax.axis_index("core")
    place = lax.broadcasted_iota(jnp.int32, (tok, tok), 0)
    query = lax.broadcasted_iota(jnp.int32, (tok, tok), 1)
    owner = seq_index + (part - 1)
    inside = jnp.logical_and(owner >= 0, owner < seq_devs)
    limit = jnp.where(inside, reach, -1)
    return jnp.abs(place - query + (part - 1) * tok) <= limit


def sort_halo(inside, outside, halo):
    core = lax.axis_index("core")

    @pl.when(core == 0)
    def _():
        halo[0] = outside[...]
        halo[1] = inside[...]

    @pl.when(core != 0)
    def _():
        halo[0] = inside[...]
        halo[1] = outside[...]


def head_probs(parts, query, reach, seq_devs):
    head, tok = query.shape
    scale = float(head) ** (-0.5)
    masks = [reached_part(p, tok, seq_devs, reach) for p in range(3)]
    scores = [
        jnp.where(masks[p], dot_first(parts[p][:head, :], query[...]) * scale, -1e30)
        for p in range(3)
    ]
    peak = functools.reduce(jnp.maximum, [jnp.max(s, axis=0, keepdims=True) for s in scores])
    weights = [jnp.where(masks[p], jnp.exp(scores[p] - peak), 0.0) for p in range(3)]
    total = sum(jnp.sum(w, axis=0, keepdims=True) for w in weights)
    inverse = 1.0 / total
    return [w * inverse for w in weights]


def own_reach(reaches):
    col_devs = lax.axis_size("zh") * lax.axis_size("x")
    col_index = lax.axis_index("zh") * lax.axis_size("x") + lax.axis_index("x")
    return reaches[lax.axis_index("row") * col_devs + col_index]


def attend_body(seq_devs, *refs):
    sources, (inside, outside, own), (send, hidden_ref) = refs[:5], refs[5:8], refs[8:10]
    query, stream, gain_row, reaches, halo, arrived = refs[10:]
    head, tok = query.shape
    cot_rows = send.at[head : 2 * head, :]
    load_all(sources, (query, stream, gain_row, reaches, cot_rows), arrived)
    sort_halo(inside, outside, halo)
    parts = (halo.at[0], own, halo.at[1])
    probs = head_probs(parts, query, own_reach(reaches), seq_devs)
    attended = sum(dot_plain(parts[p][head:, :], probs[p].astype(BF)) for p in range(3))
    hidden = (stream[...].astype(F32) + attended).astype(BF)
    hidden_ref[...] = hidden
    hidden_f = hidden.astype(F32)
    send[:head, :] = (hidden_f * column(gain_row[...])).astype(BF)
    write_tail(send, (), 2 * head, jnp.sum(hidden_f * hidden_f, axis=0, keepdims=True))


def project_body(head, slots, *refs):
    weights, (mine, theirs), (parts, feats, cots) = refs[:slots], refs[slots : slots + 2], refs[slots + 2 :]
    n_x, n_zh, _, tok = mine.shape
    units = weights[0].shape[2]
    blocks = weights[0].shape[0] // 2
    depth = n_x * n_zh * head
    squares = []
    for side, panel in enumerate((mine, theirs)):
        lanes = slice(side * tok, (side + 1) * tok)
        square = jnp.zeros((1, tok), F32)
        for zh in range(n_zh):
            for x in range(n_x):
                rows = slice((zh * n_x + x) * head, (zh * n_x + x + 1) * head)
                feats[rows, lanes] = panel[x, zh, :head, :]
                cots[rows, lanes] = panel[x, zh, head : 2 * head, :]
                square += read_tail(panel[x, zh, 2 * head :, :])
        squares.append(square)
    square = jnp.concatenate(squares, axis=1)
    for w in range(slots):
        up = weights[w][:blocks].reshape(depth, units)
        parts[w, :units, :] = dot_first(up, feats[...]).astype(BF)
        total = jnp.zeros((units, 2 * tok), F32)
        for b in range(blocks):
            total += dot_plain(weights[w][blocks + b], cots[b * BLK : (b + 1) * BLK, :])
        parts[w, units : 2 * units, :] = total.astype(BF)
        write_tail(parts, (w,), 2 * units, square)


def norm_grad_body(head, n_zh, n_x, slots, acts, *refs):
    weights, (own, send) = refs[:slots], refs[slots:]
    units = weights[0].shape[2]
    blocks = weights[0].shape[0] // 2
    tok = acts.shape[2] // 2
    per_block = BLK // head
    for b in range(blocks):
        total = jnp.zeros((BLK, 2 * tok), F32)
        for w in range(slots):
            total += dot_plain(weights[w][b], acts[w, units : 2 * units, :])
        total = total.astype(BF)
        for k in range(per_block):
            zh, x = divmod(b * per_block + k, n_x)
            rows = slice(zh * head, (zh + 1) * head)
            own[x, rows, :] = total[k * head : (k + 1) * head, :tok]
            send[x, rows, :] = total[k * head : (k + 1) * head, tok:]
    inner = sum(read_tail(acts[w, 2 * units :, :]) for w in range(slots))
    for x in range(n_x):
        write_tail(own, (x,), n_zh * head, inner[:, :tok])
        write_tail(send, (x,), n_zh * head, inner[:, tok:])


def weight_grad_body(slots, acts, feats, cots, *homes):
    units = homes[0].shape[2]
    blocks = homes[0].shape[0] // 2
    for w in range(slots):
        grad = acts[w, units : 2 * units, :]
        homes[w][:blocks] = dot_last(feats[...], grad).astype(BF).reshape(blocks, BLK, units)
        active = acts[w, :units, :]
        for b in range(blocks):
            block = dot_last(active, cots[b * BLK : (b + 1) * BLK, :])
            homes[w][blocks + b] = block.astype(BF)


def core_sum_body(rows, own, theirs, out):
    for x in range(own.shape[0]):
        total = own[x, :rows, :].astype(F32) + theirs[x, :rows, :].astype(F32)
        out[x, :rows, :] = total.astype(BF)
        write_tail(out, (x,), rows, read_tail(own[x, rows:, :]) + read_tail(theirs[x, rows:, :]))


def x_sum_body(head, pieces, out):
    n_zh = out.shape[0]
    rows = n_zh * head
    inner = sum(read_tail(pieces[x, rows:, :]) for x in range(pieces.shape[0]))
    for zh in range(n_zh):
        span = slice(zh * head, (zh + 1) * head)
        total = sum(pieces[x, span, :].astype(F32) for x in range(pieces.shape[0]))
        out[zh, :head, :] = total.astype(BF)
        write_tail(out, (zh,), head, inner)


def attend_grad_body(width_total, seq_devs, *refs):
    cot, gain_row, reaches, query, pieces, hidden, inv_rms, inside, outside, own = refs[:10]
    stream_out, query_out, inside_out, outside_out, own_out, gain_out, halo = refs[10:]
    head, tok = query.shape
    scale = float(head) ** (-0.5)
    grad_norm = sum(pieces[z, :head, :].astype(F32) for z in range(pieces.shape[0]))
    inner = sum(read_tail(pieces[z, head:, :]) for z in range(pieces.shape[0]))
    hidden_f = hidden[...].astype(F32)
    ones = jnp.ones((gain_out.shape[0], tok), F32)
    gain_out[...] = lax.dot_general(
        ones,
        grad_norm * hidden_f,
        (((1,), (1,)), ((), ())),
        precision=lax.Precision.HIGHEST,
        preferred_element_type=F32,
    )
    shrink = inv_rms[:, :tok] * inner / width_total
    grad_hidden = column(gain_row[...]) * grad_norm - hidden_f * shrink + cot[...].astype(F32)
    grad_stream = grad_hidden.astype(BF)
    stream_out[...] = grad_stream
    sort_halo(inside, outside, halo)
    parts = (halo.at[0], own, halo.at[1])
    probs = head_probs(parts, query, own_reach(reaches), seq_devs)
    grad_probs = [dot_first(parts[p][head:, :], grad_stream) for p in range(3)]
    center = sum(jnp.sum(probs[p] * grad_probs[p], axis=0, keepdims=True) for p in range(3))
    grad_query = jnp.zeros((head, tok), F32)
    for p in range(3):
        grad_scores = (probs[p] * (grad_probs[p] - center)).astype(BF)
        grad_query += dot_plain(parts[p][:head, :], grad_scores)
        key_grad = dot_last(query[...], grad_scores) * scale
        value_grad = dot_last(grad_stream, probs[p].astype(BF))
        if p == 1:
            own_out[:head, :] = key_grad
            own_out[head:, :] = value_grad
        else:
            halo[p // 2, :head, :] = key_grad.astype(BF)
            halo[p // 2, head:, :] = value_grad.astype(BF)
    query_out[...] = (grad_query * scale).astype(BF)
    core = lax.axis_index("core")

    @pl.when(core == 0)
    def _():
        outside_out[...] = halo[0]
        inside_out[...] = halo[1]

    @pl.when(core != 0)
    def _():
        inside_out[...] = halo[0]
        outside_out[...] = halo[1]


def home_sum_body(slots, *refs):
    homes, (flags, grad_up, grad_down) = refs[:slots], refs[slots:]
    blocks = homes[0].shape[0] // 2
    for b in range(2 * blocks):
        total = sum(homes[w][b].astype(F32) for w in range(slots)) * flags[b : b + 1, :]
        if b < blocks:
            grad_up[b * BLK : (b + 1) * BLK, :] = total.astype(BF)
        else:
            grad_down[:, (b - blocks) * BLK : (b - blocks + 1) * BLK] = total.astype(BF)


def pair_sum_body(own, inside, outside, gains, key_out, value_out, gain_out):
    head = key_out.shape[0]
    gain_out[...] = jnp.sum(gains[...], axis=0, keepdims=True)
    total = (own[...] + inside[...].astype(F32) + outside[...].astype(F32)).astype(BF)
    key_out[...] = total[:head, :]
    value_out[...] = total[head:, :]


def on_device(
    stream,
    query_heads,
    key_heads,
    value_heads,
    windows,
    norm_gain,
    up_weight,
    down_weight,
    up_rows,
    up_cols,
    down_rows,
    down_cols,
    cotangent,
):
    tok, head = stream.shape
    n_zl, n_core, n_row, n_zh, n_x = (lax.axis_size(a) for a in ("zl", "core", "row", "zh", "x"))
    seq_devs = n_zl * n_core
    col_devs = n_zh * n_x
    row_index = lax.axis_index("row")
    col_index = lax.axis_index(("zh", "x"))
    width_total = head * n_row * col_devs
    depth, units = up_weight.shape
    blocks = depth // BLK
    both_toks = n_core * tok
    swap = [(i, n_core - 1 - i) for i in range(n_core)]
    cross = [(i, i + 1) for i in range(1, seq_devs - 1, 2)]
    cross += [(j, i) for i, j in cross]
    query_t, stream_t, cot_t = query_heads.T, stream.T, cotangent.T
    gain = norm_gain[None, :]

    ids = [a.reshape(-1, BLK) for a in (up_rows, up_cols, down_cols, down_rows)]
    both, flags, paired = call_kernel(
        functools.partial(prepare_body, blocks),
        [
            shaped((2 * blocks, BLK, units), BF),
            shaped((2 * blocks, BLK), F32),
            shaped((2 * head, tok), BF),
        ],
        0,
        up_weight,
        down_weight,
        *ids,
        key_heads.T,
        value_heads.T,
        loads=8,
        scratch=[held(a) for a in (up_weight, down_weight, *ids)],
    )
    inside = lax.ppermute(paired, "core", swap)
    outside = lax.ppermute(paired, ("zl", "core"), cross)

    halo = pltpu.VMEM((2, 2 * head, tok), BF)
    reaches = pltpu.SMEM(windows.shape, windows.dtype)
    send, hidden = call_kernel(
        functools.partial(attend_body, seq_devs),
        [shaped((2 * head + TAIL, tok), BF), shaped((head, tok), BF)],
        12 * tok * tok * head,
        query_t,
        stream_t,
        gain,
        windows,
        cot_t,
        inside,
        outside,
        paired,
        loads=5,
        scratch=[held(query_t), held(stream_t), held(gain), reaches, halo],
    )
    near = [window_send(both, w, n_zh, n_zl, n_core, False) for w in (1, 3)]

    panel = lax.all_gather(send, "zh", axis=0, tiled=False)
    panel, near = lax.optimization_barrier((panel, near))
    far = window_send(near[0], 1, n_zh, n_zl, n_core, False)
    panel = spread(panel, "x")
    panel, far = lax.optimization_barrier((panel, far))
    other = lax.ppermute(panel, "core", swap)
    slots = [far, near[0], both, near[1]]

    parts, feats, cots = call_kernel(
        functools.partial(project_body, head, n_zl),
        [
            shaped((n_zl, 2 * units + TAIL, both_toks), BF),
            shaped((depth, both_toks), BF),
            shaped((depth, both_toks), BF),
        ],
        4 * n_zl * depth * units * both_toks,
        *slots,
        panel,
        other,
    )
    parts = exchange(parts, "row")
    summed = jnp.sum(parts[:, : 2 * units].astype(F32), axis=0)
    square_total = jnp.sum(tail_value(parts[:, 2 * units :]), axis=0)
    inv_rms = lax.rsqrt(square_total / width_total + EPSILON)
    pre_act = summed[:units] * inv_rms
    activation = gelu_value(pre_act).astype(BF)
    grad_act = (summed[units:] * gelu_slope(pre_act) * inv_rms).astype(BF)
    inner_part = jnp.sum(grad_act.astype(F32) * pre_act, axis=0)
    acts = spread(jnp.concatenate([activation, grad_act, tail_rows(inner_part)], axis=0), "row")

    mine, theirs = call_kernel(
        functools.partial(norm_grad_body, head, n_zh, n_x, n_zl),
        [shaped((n_x, n_zh * head + TAIL, tok), BF)] * 2,
        2 * n_zl * depth * units * both_toks,
        acts,
        *slots,
    )
    theirs = lax.ppermute(theirs, "core", swap)
    homes = call_kernel(
        functools.partial(weight_grad_body, n_zl),
        [shaped((2 * blocks, BLK, units), BF)] * n_zl,
        4 * n_zl * depth * units * both_toks,
        acts,
        feats,
        cots,
    )
    pieces = call_kernel(
        functools.partial(core_sum_body, n_zh * head),
        [shaped((n_x, n_zh * head + TAIL, tok), BF)],
        0,
        mine,
        theirs,
    )[0]
    pieces = exchange(pieces, "x")
    pieces = call_kernel(
        functools.partial(x_sum_body, head),
        [shaped((n_zh, head + TAIL, tok), BF)],
        0,
        pieces,
    )[0]
    far = window_send(homes[0], 1, n_zh, n_zl, n_core, True)
    near = window_send(homes[3], 3, n_zh, n_zl, n_core, True)
    pieces, far = lax.optimization_barrier((pieces, far))
    far = (homes[1].astype(F32) + far.astype(F32)).astype(BF)
    far = window_send(far, 1, n_zh, n_zl, n_core, True)
    pieces = exchange(pieces, "zh")
    grad_stream, grad_query, inside_grad, outside_grad, own, gain_parts = call_kernel(
        functools.partial(attend_grad_body, width_total, seq_devs),
        [
            shaped((head, tok), BF),
            shaped((head, tok), BF),
            shaped((2 * head, tok), BF),
            shaped((2 * head, tok), BF),
            shaped((2 * head, tok), F32),
            shaped((seq_devs, head), F32),
        ],
        30 * tok * tok * head,
        cot_t,
        gain,
        windows,
        query_t,
        pieces,
        hidden,
        inv_rms[None],
        inside,
        outside,
        paired,
        scratch=[halo],
    )
    gain_parts, far, near = lax.optimization_barrier((gain_parts, far, near))
    gain_parts = exchange(gain_parts, ("zl", "core"))
    inside_grad = lax.ppermute(inside_grad, "core", swap)
    outside_grad = lax.ppermute(outside_grad, ("zl", "core"), cross)
    grad_up, grad_down = call_kernel(
        functools.partial(home_sum_body, 3),
        [shaped((depth, units), BF), shaped((units, depth), BF)],
        0,
        far,
        near,
        homes[2],
        flags,
    )
    grad_key, grad_value, grad_gain = call_kernel(
        pair_sum_body,
        [shaped((head, tok), BF), shaped((head, tok), BF), shaped((1, head), F32)],
        0,
        own,
        inside_grad,
        outside_grad,
        gain_parts,
    )
    grad_gain = grad_gain.reshape(head)
    return (
        grad_stream.T,
        grad_query.T,
        grad_key.T,
        grad_value.T,
        grad_gain,
        grad_up,
        grad_down,
    )


def solution(mesh):
    seq, row, col = (mesh.shape[a] for a in ("seq", "row", "col"))
    fine = Mesh(
        mesh.devices.reshape(seq // 2, 2, row, 4, col // 4), ("zl", "core", "row", "zh", "x")
    )
    features = P(("zl", "core"), ("row", "zh", "x"))
    gain_spec = P(("row", "zh", "x"))
    up_spec = P("row", ("zl", "core", "zh", "x"))
    down_spec = P(("zl", "core", "zh", "x"), "row")
    in_specs = (
        (features,) * 4 + (P(), gain_spec, up_spec, down_spec) + (P(),) * 4 + (features,)
    )
    out_specs = (features,) * 4 + (gain_spec, up_spec, down_spec)
    return jax.shard_map(
        on_device, mesh=fine, in_specs=in_specs, out_specs=out_specs, check_vma=False
    )
```

```python
import functools

import jax
import jax.numpy as jnp
from jax import lax
from jax.experimental import pallas as pl
from jax.experimental.pallas import tpu as pltpu
from jax.sharding import Mesh
from jax.sharding import PartitionSpec as P

BLK = 128
GELU_C = 0.7978845608028654
GELU_A = 0.044715
EPSILON = 1e-05
TAIL = 16
BF = jnp.bfloat16
F32 = jnp.float32


def gelu_value(pre_act):
    tanh_arg = GELU_C * (pre_act + GELU_A * pre_act * pre_act * pre_act)
    return 0.5 * pre_act * (1.0 + jnp.tanh(tanh_arg))


def gelu_slope(pre_act):
    tanh_arg = GELU_C * (pre_act + GELU_A * pre_act * pre_act * pre_act)
    tanh_val = jnp.tanh(tanh_arg)
    return 0.5 * (1.0 + tanh_val) + 0.5 * pre_act * (1.0 - tanh_val * tanh_val) * GELU_C * (
        1.0 + 3.0 * GELU_A * pre_act * pre_act
    )


def tail_rows(vector):
    high = lax.reduce_precision(vector, 8, 7)
    low = vector - high
    pair = jnp.stack([high, low]).astype(BF)
    return jnp.pad(pair, ((0, TAIL - 2), (0, 0)))


def tail_value(rows):
    return rows[..., 0, :].astype(F32) + rows[..., 1, :].astype(F32)


def spread(array, axis):
    count = lax.axis_size(axis)
    copies = jnp.broadcast_to(array[None], (count,) + array.shape)
    return lax.all_to_all(copies, axis, 0, 0, tiled=True)


def exchange(pieces, axis):
    return lax.all_to_all(pieces, axis, 0, 0, tiled=True)


def window_send(array, slot, n_zh, n_zl, n_core, home):
    ring = n_zh * n_zl
    pairs = []
    for place in range(ring):
        for core in range(n_core):
            step = (slot - n_zl // 2) * (1 if core == 0 else -1)
            owner, worker = (
                ((z % n_zl) * n_core + core) * n_zh + z // n_zl for z in ((place + step) % ring, place)
            )
            pairs.append((worker, owner) if home else (owner, worker))
    if all(source == target for source, target in pairs):
        return array
    return lax.ppermute(array, ("zl", "core", "zh"), pairs)


def call_kernel(body, out_shapes, flops, *operands, loads=0, scratch=()):
    moved = sum(a.size * a.dtype.itemsize for a in operands)
    moved += sum(a.size * a.dtype.itemsize for a in out_shapes)
    vmem = pl.BlockSpec(memory_space=pltpu.VMEM)
    smem = pl.BlockSpec(memory_space=pltpu.SMEM)
    return pl.pallas_call(
        body,
        out_shape=out_shapes,
        in_specs=[pl.BlockSpec(memory_space=pltpu.HBM)] * loads
        + [smem if a.ndim == 1 else vmem for a in operands[loads:]],
        out_specs=[vmem] * len(out_shapes),
        scratch_shapes=list(scratch) + ([pltpu.SemaphoreType.DMA((loads,))] if loads else []),
        compiler_params=pltpu.CompilerParams(vmem_limit_bytes=(60 if loads else 24) * 1024 * 1024),
        cost_estimate=pl.CostEstimate(flops=flops, bytes_accessed=moved, transcendentals=0),
    )(*operands)


def load_all(sources, targets, arrived):
    copies = [
        pltpu.make_async_copy(source, target, arrived.at[i])
        for i, (source, target) in enumerate(zip(sources, targets, strict=True))
    ]
    for copy in copies:
        copy.start()
    for copy in copies:
        copy.wait()


def held(array):
    return pltpu.VMEM(array.shape, array.dtype)


def shaped(shape, dtype):
    return jax.ShapeDtypeStruct(shape, dtype)


def dot_first(left, right):
    return lax.dot_general(left, right, (((0,), (0,)), ((), ())), preferred_element_type=F32)


def dot_last(left, right):
    return lax.dot_general(left, right, (((1,), (1,)), ((), ())), preferred_element_type=F32)


def dot_plain(left, right):
    return jnp.dot(left, right, preferred_element_type=F32)


def write_tail(ref, index, first, vector):
    high = vector.astype(BF)
    low = (vector - high.astype(F32)).astype(BF)
    place = lax.broadcasted_iota(jnp.int32, (TAIL, vector.shape[1]), 0)
    rows = jnp.where(place == 0, high.astype(F32), jnp.where(place == 1, low.astype(F32), 0.0))
    ref[index + (slice(first, first + TAIL), slice(None))] = rows.astype(BF)


def read_tail(rows):
    rows = rows.astype(F32)
    return rows[0:1] + rows[1:2]


def prepare_body(blocks, *refs):
    sources, (both_ref, flag_ref, pair_ref) = refs[:8], refs[8:11]
    up_ref, down_ref, up_in, up_out, down_in, down_out, arrived = refs[11:]
    head = sources[6].shape[0]
    pair_halves = (pair_ref.at[:head, :], pair_ref.at[head:, :])
    load_all(sources, (up_ref, down_ref, up_in, up_out, down_in, down_out) + pair_halves, arrived)
    col_devs = lax.axis_size("zh") * lax.axis_size("x")
    seq_index = lax.axis_index("zl") * lax.axis_size("core") + lax.axis_index("core")
    col_index = lax.axis_index("zh") * lax.axis_size("x") + lax.axis_index("x")
    own_block = seq_index * col_devs + col_index
    first = lax.axis_index("row") * blocks
    for kind, (inner, outer) in enumerate(((up_in, up_out), (down_in, down_out))):
        shifted = jnp.where(outer[...] == own_block, inner[...] - first, -1)
        for b in range(blocks):
            hit = jnp.where(shifted == b, 1.0, 0.0)
            flag = jnp.max(jnp.max(hit, axis=0, keepdims=True), axis=1, keepdims=True)
            flag_ref[kind * blocks + b : kind * blocks + b + 1, :] = jnp.broadcast_to(flag, (1, BLK))
            if kind == 0:
                block = up_ref[b * BLK : (b + 1) * BLK, :]
            else:
                block = down_ref[:, b * BLK : (b + 1) * BLK]
            both_ref[kind * blocks + b] = (block.astype(F32) * flag).astype(BF)


def column(row):
    count = row.shape[1]
    across = lax.broadcasted_iota(jnp.int32, (count, count), 1)
    down = lax.broadcasted_iota(jnp.int32, (count, count), 0)
    return jnp.sum(jnp.where(across == down, row, 0.0), axis=1, keepdims=True)


def reached_part(part, tok, seq_devs, reach):
    seq_index = lax.axis_index("zl") * lax.axis_size("core") + lax.axis_index("core")
    place = lax.broadcasted_iota(jnp.int32, (tok, tok), 0)
    query = lax.broadcasted_iota(jnp.int32, (tok, tok), 1)
    owner = seq_index + (part - 1)
    inside = jnp.logical_and(owner >= 0, owner < seq_devs)
    limit = jnp.where(inside, reach, -1)
    return jnp.abs(place - query + (part - 1) * tok) <= limit


def sort_halo(inside, outside, halo):
    core = lax.axis_index("core")

    @pl.when(core == 0)
    def _():
        halo[0] = outside[...]
        halo[1] = inside[...]

    @pl.when(core != 0)
    def _():
        halo[0] = inside[...]
        halo[1] = outside[...]


def head_probs(parts, query, reach, seq_devs):
    head, tok = query.shape
    scale = float(head) ** (-0.5)
    masks = [reached_part(p, tok, seq_devs, reach) for p in range(3)]
    scores = [
        jnp.where(masks[p], dot_first(parts[p][:head, :], query[...]) * scale, -1e30)
        for p in range(3)
    ]
    peak = functools.reduce(jnp.maximum, [jnp.max(s, axis=0, keepdims=True) for s in scores])
    weights = [jnp.where(masks[p], jnp.exp(scores[p] - peak), 0.0) for p in range(3)]
    total = sum(jnp.sum(w, axis=0, keepdims=True) for w in weights)
    inverse = 1.0 / total
    return [w * inverse for w in weights]


def own_reach(reaches):
    col_devs = lax.axis_size("zh") * lax.axis_size("x")
    col_index = lax.axis_index("zh") * lax.axis_size("x") + lax.axis_index("x")
    return reaches[lax.axis_index("row") * col_devs + col_index]


def attend_body(seq_devs, *refs):
    sources, (inside, outside, own), (send, hidden_ref) = refs[:5], refs[5:8], refs[8:10]
    query, stream, gain_row, reaches, halo, arrived = refs[10:]
    head, tok = query.shape
    cot_rows = send.at[head : 2 * head, :]
    load_all(sources, (query, stream, gain_row, reaches, cot_rows), arrived)
    sort_halo(inside, outside, halo)
    parts = (halo.at[0], own, halo.at[1])
    probs = head_probs(parts, query, own_reach(reaches), seq_devs)
    attended = sum(dot_plain(parts[p][head:, :], probs[p].astype(BF)) for p in range(3))
    hidden = (stream[...].astype(F32) + attended).astype(BF)
    hidden_ref[...] = hidden
    hidden_f = hidden.astype(F32)
    send[:head, :] = (hidden_f * column(gain_row[...])).astype(BF)
    write_tail(send, (), 2 * head, jnp.sum(hidden_f * hidden_f, axis=0, keepdims=True))


def project_body(head, slots, *refs):
    weights, (mine, theirs), (parts, feats, cots) = refs[:slots], refs[slots : slots + 2], refs[slots + 2 :]
    n_x, n_zh, _, tok = mine.shape
    units = weights[0].shape[2]
    blocks = weights[0].shape[0] // 2
    depth = n_x * n_zh * head
    squares = []
    for side, panel in enumerate((mine, theirs)):
        lanes = slice(side * tok, (side + 1) * tok)
        square = jnp.zeros((1, tok), F32)
        for zh in range(n_zh):
            for x in range(n_x):
                rows = slice((zh * n_x + x) * head, (zh * n_x + x + 1) * head)
                feats[rows, lanes] = panel[x, zh, :head, :]
                cots[rows, lanes] = panel[x, zh, head : 2 * head, :]
                square += read_tail(panel[x, zh, 2 * head :, :])
        squares.append(square)
    square = jnp.concatenate(squares, axis=1)
    for w in range(slots):
        up = weights[w][:blocks].reshape(depth, units)
        parts[w, :units, :] = dot_first(up, feats[...]).astype(BF)
        total = jnp.zeros((units, 2 * tok), F32)
        for b in range(blocks):
            total += dot_plain(weights[w][blocks + b], cots[b * BLK : (b + 1) * BLK, :])
        parts[w, units : 2 * units, :] = total.astype(BF)
        write_tail(parts, (w,), 2 * units, square)


def norm_grad_body(head, n_zh, n_x, slots, acts, *refs):
    weights, out = refs[:slots], refs[slots]
    units = weights[0].shape[2]
    blocks = weights[0].shape[0] // 2
    tok = acts.shape[2] // 2
    per_block = BLK // head
    own = lax.axis_index("core") * n_x
    other = (1 - lax.axis_index("core")) * n_x
    for b in range(blocks):
        total = jnp.zeros((BLK, 2 * tok), F32)
        for w in range(slots):
            total += dot_plain(weights[w][b], acts[w, units : 2 * units, :])
        total = total.astype(BF)
        for k in range(per_block):
            zh, x = divmod(b * per_block + k, n_x)
            rows = slice(zh * head, (zh + 1) * head)
            out[own + x, rows, :] = total[k * head : (k + 1) * head, :tok]
            out[other + x, rows, :] = total[k * head : (k + 1) * head, tok:]
    inner = sum(read_tail(acts[w, 2 * units :, :]) for w in range(slots))
    for x in range(n_x):
        write_tail(out, (own + x,), n_zh * head, inner[:, :tok])
        write_tail(out, (other + x,), n_zh * head, inner[:, tok:])


def weight_grad_body(slots, acts, feats, cots, *homes):
    units = homes[0].shape[2]
    blocks = homes[0].shape[0] // 2
    for w in range(slots):
        grad = acts[w, units : 2 * units, :]
        homes[w][:blocks] = dot_last(feats[...], grad).astype(BF).reshape(blocks, BLK, units)
        active = acts[w, :units, :]
        for b in range(blocks):
            block = dot_last(active, cots[b * BLK : (b + 1) * BLK, :])
            homes[w][blocks + b] = block.astype(BF)


def x_sum_body(head, pieces, out):
    n_zh = out.shape[0]
    rows = n_zh * head
    inner = sum(read_tail(pieces[x, rows:, :]) for x in range(pieces.shape[0]))
    for zh in range(n_zh):
        span = slice(zh * head, (zh + 1) * head)
        total = sum(pieces[x, span, :].astype(F32) for x in range(pieces.shape[0]))
        out[zh, :head, :] = total.astype(BF)
        write_tail(out, (zh,), head, inner)


def probs_body(seq_devs, reaches, query, inside, outside, own, probs_ref, halo):
    sort_halo(inside, outside, halo)
    probs = head_probs((halo.at[0], own, halo.at[1]), query, own_reach(reaches), seq_devs)
    for p in range(3):
        probs_ref[p] = probs[p]


def attend_grad_body(width_total, *refs):
    cot, gain_row, probs, query, pieces, hidden, inv_rms, inside, outside, own = refs[:10]
    stream_out, query_out, inside_out, outside_out, own_out, gain_out, halo = refs[10:]
    head, tok = query.shape
    scale = float(head) ** (-0.5)
    grad_norm = sum(pieces[z, :head, :].astype(F32) for z in range(pieces.shape[0]))
    inner = sum(read_tail(pieces[z, head:, :]) for z in range(pieces.shape[0]))
    hidden_f = hidden[...].astype(F32)
    ones = jnp.ones((gain_out.shape[0], tok), F32)
    gain_out[...] = lax.dot_general(
        ones,
        grad_norm * hidden_f,
        (((1,), (1,)), ((), ())),
        precision=lax.Precision.HIGHEST,
        preferred_element_type=F32,
    )
    shrink = inv_rms[:, :tok] * inner / width_total
    grad_hidden = column(gain_row[...]) * grad_norm - hidden_f * shrink + cot[...].astype(F32)
    grad_stream = grad_hidden.astype(BF)
    stream_out[...] = grad_stream
    sort_halo(inside, outside, halo)
    parts = (halo.at[0], own, halo.at[1])
    grad_probs = [dot_first(parts[p][head:, :], grad_stream) for p in range(3)]
    center = sum(jnp.sum(probs[p] * grad_probs[p], axis=0, keepdims=True) for p in range(3))
    grad_query = jnp.zeros((head, tok), F32)
    for p in range(3):
        grad_scores = (probs[p] * (grad_probs[p] - center)).astype(BF)
        grad_query += dot_plain(parts[p][:head, :], grad_scores)
        key_grad = dot_last(query[...], grad_scores) * scale
        value_grad = dot_last(grad_stream, probs[p].astype(BF))
        if p == 1:
            own_out[:head, :] = key_grad
            own_out[head:, :] = value_grad
        else:
            halo[p // 2, :head, :] = key_grad.astype(BF)
            halo[p // 2, head:, :] = value_grad.astype(BF)
    query_out[...] = (grad_query * scale).astype(BF)
    core = lax.axis_index("core")

    @pl.when(core == 0)
    def _():
        outside_out[...] = halo[0]
        inside_out[...] = halo[1]

    @pl.when(core != 0)
    def _():
        inside_out[...] = halo[0]
        outside_out[...] = halo[1]


def home_sum_body(slots, *refs):
    homes, (flags, grad_up, grad_down) = refs[:slots], refs[slots:]
    blocks = homes[0].shape[0] // 2
    for b in range(2 * blocks):
        total = sum(homes[w][b].astype(F32) for w in range(slots)) * flags[b : b + 1, :]
        if b < blocks:
            grad_up[b * BLK : (b + 1) * BLK, :] = total.astype(BF)
        else:
            grad_down[:, (b - blocks) * BLK : (b - blocks + 1) * BLK] = total.astype(BF)


def pair_sum_body(own, inside, outside, gains, key_out, value_out, gain_out):
    head = key_out.shape[0]
    gain_out[...] = jnp.sum(gains[...], axis=0, keepdims=True)
    total = (own[...] + inside[...].astype(F32) + outside[...].astype(F32)).astype(BF)
    key_out[...] = total[:head, :]
    value_out[...] = total[head:, :]


def on_device(
    stream,
    query_heads,
    key_heads,
    value_heads,
    windows,
    norm_gain,
    up_weight,
    down_weight,
    up_rows,
    up_cols,
    down_rows,
    down_cols,
    cotangent,
):
    tok, head = stream.shape
    n_zl, n_core, n_row, n_zh, n_x = (lax.axis_size(a) for a in ("zl", "core", "row", "zh", "x"))
    seq_devs = n_zl * n_core
    col_devs = n_zh * n_x
    row_index = lax.axis_index("row")
    col_index = lax.axis_index(("zh", "x"))
    width_total = head * n_row * col_devs
    depth, units = up_weight.shape
    blocks = depth // BLK
    both_toks = n_core * tok
    swap = [(i, n_core - 1 - i) for i in range(n_core)]
    cross = [(i, i + 1) for i in range(1, seq_devs - 1, 2)]
    cross += [(j, i) for i, j in cross]
    query_t, stream_t, cot_t = query_heads.T, stream.T, cotangent.T
    gain = norm_gain[None, :]

    ids = [a.reshape(-1, BLK) for a in (up_rows, up_cols, down_cols, down_rows)]
    both, flags, paired = call_kernel(
        functools.partial(prepare_body, blocks),
        [
            shaped((2 * blocks, BLK, units), BF),
            shaped((2 * blocks, BLK), F32),
            shaped((2 * head, tok), BF),
        ],
        0,
        up_weight,
        down_weight,
        *ids,
        key_heads.T,
        value_heads.T,
        loads=8,
        scratch=[held(a) for a in (up_weight, down_weight, *ids)],
    )
    inside = lax.ppermute(paired, "core", swap)
    outside = lax.ppermute(paired, ("zl", "core"), cross)

    halo = pltpu.VMEM((2, 2 * head, tok), BF)
    reaches = pltpu.SMEM(windows.shape, windows.dtype)
    send, hidden = call_kernel(
        functools.partial(attend_body, seq_devs),
        [shaped((2 * head + TAIL, tok), BF), shaped((head, tok), BF)],
        12 * tok * tok * head,
        query_t,
        stream_t,
        gain,
        windows,
        cot_t,
        inside,
        outside,
        paired,
        loads=5,
        scratch=[held(query_t), held(stream_t), held(gain), reaches, halo],
    )
    far = window_send(both, 0, n_zh, n_zl, n_core, False)

    panel = lax.all_gather(send, "zh", axis=0, tiled=False)
    panel, far, both = lax.optimization_barrier((panel, far, both))
    near = [window_send(both, w, n_zh, n_zl, n_core, False) for w in (1, 3)]
    panel = spread(panel, "x")
    panel, near = lax.optimization_barrier((panel, near))
    other = lax.ppermute(panel, "core", swap)
    slots = [far, near[0], both, near[1]]

    parts, feats, cots = call_kernel(
        functools.partial(project_body, head, n_zl),
        [
            shaped((n_zl, 2 * units + TAIL, both_toks), BF),
            shaped((depth, both_toks), BF),
            shaped((depth, both_toks), BF),
        ],
        4 * n_zl * depth * units * both_toks,
        *slots,
        panel,
        other,
    )
    parts = exchange(parts, "row")
    summed = jnp.sum(parts[:, : 2 * units].astype(F32), axis=0)
    square_total = jnp.sum(tail_value(parts[:, 2 * units :]), axis=0)
    inv_rms = lax.rsqrt(square_total / width_total + EPSILON)
    pre_act = summed[:units] * inv_rms
    activation = gelu_value(pre_act).astype(BF)
    grad_act = (summed[units:] * gelu_slope(pre_act) * inv_rms).astype(BF)
    inner_part = jnp.sum(grad_act.astype(F32) * pre_act, axis=0)
    acts = spread(jnp.concatenate([activation, grad_act, tail_rows(inner_part)], axis=0), "row")

    pieces = call_kernel(
        functools.partial(norm_grad_body, head, n_zh, n_x, n_zl),
        [shaped((n_core * n_x, n_zh * head + TAIL, tok), BF)],
        2 * n_zl * depth * units * both_toks,
        acts,
        *slots,
    )[0]
    homes = call_kernel(
        functools.partial(weight_grad_body, n_zl),
        [shaped((2 * blocks, BLK, units), BF)] * n_zl,
        4 * n_zl * depth * units * both_toks,
        acts,
        feats,
        cots,
    )
    pieces = exchange(pieces, ("core", "x"))
    pieces = call_kernel(
        functools.partial(x_sum_body, head),
        [shaped((n_zh, head + TAIL, tok), BF)],
        0,
        pieces,
    )[0]
    early = [window_send(homes[w], w, n_zh, n_zl, n_core, True) for w in (0, 1)]
    late = window_send(homes[3], 3, n_zh, n_zl, n_core, True)
    query_t, feats = lax.optimization_barrier((query_t, feats))
    probs = call_kernel(
        functools.partial(probs_body, seq_devs),
        [shaped((3, tok, tok), F32)],
        4 * 10**9,
        windows,
        query_t,
        inside,
        outside,
        paired,
        scratch=[halo],
    )[0]
    pieces = exchange(pieces, "zh")
    pieces, early = lax.optimization_barrier((pieces, early))

    grad_stream, grad_query, inside_grad, outside_grad, own, gain_parts = call_kernel(
        functools.partial(attend_grad_body, width_total),
        [
            shaped((head, tok), BF),
            shaped((head, tok), BF),
            shaped((2 * head, tok), BF),
            shaped((2 * head, tok), BF),
            shaped((2 * head, tok), F32),
            shaped((seq_devs, head), F32),
        ],
        30 * tok * tok * head,
        cot_t,
        gain,
        probs,
        query_t,
        pieces,
        hidden,
        inv_rms[None],
        inside,
        outside,
        paired,
        scratch=[halo],
    )
    own, late = lax.optimization_barrier((own, late))
    gain_parts = exchange(gain_parts, ("zl", "core"))
    inside_grad = lax.ppermute(inside_grad, "core", swap)
    outside_grad = lax.ppermute(outside_grad, ("zl", "core"), cross)
    grad_up, grad_down = call_kernel(
        functools.partial(home_sum_body, n_zl),
        [shaped((depth, units), BF), shaped((units, depth), BF)],
        0,
        *early,
        late,
        homes[2],
        flags,
    )
    grad_key, grad_value, grad_gain = call_kernel(
        pair_sum_body,
        [shaped((head, tok), BF), shaped((head, tok), BF), shaped((1, head), F32)],
        0,
        own,
        inside_grad,
        outside_grad,
        gain_parts,
    )
    grad_gain = grad_gain.reshape(head)
    return (
        grad_stream.T,
        grad_query.T,
        grad_key.T,
        grad_value.T,
        grad_gain,
        grad_up,
        grad_down,
    )


def solution(mesh):
    seq, row, col = (mesh.shape[a] for a in ("seq", "row", "col"))
    fine = Mesh(
        mesh.devices.reshape(seq // 2, 2, row, 4, col // 4), ("zl", "core", "row", "zh", "x")
    )
    features = P(("zl", "core"), ("row", "zh", "x"))
    gain_spec = P(("row", "zh", "x"))
    up_spec = P("row", ("zl", "core", "zh", "x"))
    down_spec = P(("zl", "core", "zh", "x"), "row")
    in_specs = (
        (features,) * 4 + (P(), gain_spec, up_spec, down_spec) + (P(),) * 4 + (features,)
    )
    out_specs = (features,) * 4 + (gain_spec, up_spec, down_spec)
    return jax.shard_map(
        on_device, mesh=fine, in_specs=in_specs, out_specs=out_specs, check_vma=False
    )
```

```python
import functools

import jax
import jax.numpy as jnp
from jax import lax
from jax.experimental import pallas as pl
from jax.experimental.pallas import tpu as pltpu
from jax.sharding import Mesh
from jax.sharding import PartitionSpec as P

BLK = 128
GELU_C = 0.7978845608028654
GELU_A = 0.044715
EPSILON = 1e-05
TAIL = 16
BF = jnp.bfloat16
F32 = jnp.float32


def gelu_value(pre_act):
    tanh_arg = GELU_C * (pre_act + GELU_A * pre_act * pre_act * pre_act)
    return 0.5 * pre_act * (1.0 + jnp.tanh(tanh_arg))


def gelu_slope(pre_act):
    tanh_arg = GELU_C * (pre_act + GELU_A * pre_act * pre_act * pre_act)
    tanh_val = jnp.tanh(tanh_arg)
    return 0.5 * (1.0 + tanh_val) + 0.5 * pre_act * (1.0 - tanh_val * tanh_val) * GELU_C * (
        1.0 + 3.0 * GELU_A * pre_act * pre_act
    )


def tail_rows(vector):
    high = lax.reduce_precision(vector, 8, 7)
    low = vector - high
    pair = jnp.stack([high, low]).astype(BF)
    return jnp.pad(pair, ((0, TAIL - 2), (0, 0)))


def tail_value(rows):
    return rows[..., 0, :].astype(F32) + rows[..., 1, :].astype(F32)


def spread(array, axis):
    count = lax.axis_size(axis)
    copies = jnp.broadcast_to(array[None], (count,) + array.shape)
    return lax.all_to_all(copies, axis, 0, 0, tiled=True)


def exchange(pieces, axis):
    return lax.all_to_all(pieces, axis, 0, 0, tiled=True)


def window_send(array, slot, n_zh, n_zl, n_core, home):
    ring = n_zh * n_zl
    pairs = []
    for place in range(ring):
        for core in range(n_core):
            step = (slot - n_zl // 2) * (1 if core == 0 else -1)
            owner, worker = (
                ((z % n_zl) * n_core + core) * n_zh + z // n_zl for z in ((place + step) % ring, place)
            )
            pairs.append((worker, owner) if home else (owner, worker))
    if all(source == target for source, target in pairs):
        return array
    return lax.ppermute(array, ("zl", "core", "zh"), pairs)


def call_kernel(body, out_shapes, flops, *operands, loads=0, scratch=()):
    moved = sum(a.size * a.dtype.itemsize for a in operands)
    moved += sum(a.size * a.dtype.itemsize for a in out_shapes)
    vmem = pl.BlockSpec(memory_space=pltpu.VMEM)
    smem = pl.BlockSpec(memory_space=pltpu.SMEM)
    return pl.pallas_call(
        body,
        out_shape=out_shapes,
        in_specs=[pl.BlockSpec(memory_space=pltpu.HBM)] * loads
        + [smem if a.ndim == 1 else vmem for a in operands[loads:]],
        out_specs=[vmem] * len(out_shapes),
        scratch_shapes=list(scratch) + ([pltpu.SemaphoreType.DMA((loads,))] if loads else []),
        compiler_params=pltpu.CompilerParams(vmem_limit_bytes=(60 if loads else 24) * 1024 * 1024),
        cost_estimate=pl.CostEstimate(flops=flops, bytes_accessed=moved, transcendentals=0),
    )(*operands)


def load_all(sources, targets, arrived):
    copies = [
        pltpu.make_async_copy(source, target, arrived.at[i])
        for i, (source, target) in enumerate(zip(sources, targets, strict=True))
    ]
    for copy in copies:
        copy.start()
    for copy in copies:
        copy.wait()


def held(array):
    return pltpu.VMEM(array.shape, array.dtype)


def shaped(shape, dtype):
    return jax.ShapeDtypeStruct(shape, dtype)


def dot_first(left, right):
    return lax.dot_general(left, right, (((0,), (0,)), ((), ())), preferred_element_type=F32)


def dot_last(left, right):
    return lax.dot_general(left, right, (((1,), (1,)), ((), ())), preferred_element_type=F32)


def dot_plain(left, right):
    return jnp.dot(left, right, preferred_element_type=F32)


def write_tail(ref, index, first, vector):
    high = vector.astype(BF)
    low = (vector - high.astype(F32)).astype(BF)
    place = lax.broadcasted_iota(jnp.int32, (TAIL, vector.shape[1]), 0)
    rows = jnp.where(place == 0, high.astype(F32), jnp.where(place == 1, low.astype(F32), 0.0))
    ref[index + (slice(first, first + TAIL), slice(None))] = rows.astype(BF)


def read_tail(rows):
    rows = rows.astype(F32)
    return rows[0:1] + rows[1:2]


def prepare_body(blocks, *refs):
    sources, (both_ref, flag_ref, pair_ref) = refs[:8], refs[8:11]
    up_ref, down_ref, up_in, up_out, down_in, down_out, arrived = refs[11:]
    head = sources[6].shape[0]
    pair_halves = (pair_ref.at[:head, :], pair_ref.at[head:, :])
    load_all(sources, (up_ref, down_ref, up_in, up_out, down_in, down_out) + pair_halves, arrived)
    col_devs = lax.axis_size("zh") * lax.axis_size("x")
    seq_index = lax.axis_index("zl") * lax.axis_size("core") + lax.axis_index("core")
    col_index = lax.axis_index("zh") * lax.axis_size("x") + lax.axis_index("x")
    own_block = seq_index * col_devs + col_index
    first = lax.axis_index("row") * blocks
    for kind, (inner, outer) in enumerate(((up_in, up_out), (down_in, down_out))):
        shifted = jnp.where(outer[...] == own_block, inner[...] - first, -1)
        for b in range(blocks):
            hit = jnp.where(shifted == b, 1.0, 0.0)
            flag = jnp.max(jnp.max(hit, axis=0, keepdims=True), axis=1, keepdims=True)
            flag_ref[kind * blocks + b : kind * blocks + b + 1, :] = jnp.broadcast_to(flag, (1, BLK))
            if kind == 0:
                block = up_ref[b * BLK : (b + 1) * BLK, :]
            else:
                block = down_ref[:, b * BLK : (b + 1) * BLK]
            both_ref[kind * blocks + b] = (block.astype(F32) * flag).astype(BF)


def column(row):
    count = row.shape[1]
    across = lax.broadcasted_iota(jnp.int32, (count, count), 1)
    down = lax.broadcasted_iota(jnp.int32, (count, count), 0)
    return jnp.sum(jnp.where(across == down, row, 0.0), axis=1, keepdims=True)


def reached_part(part, tok, seq_devs, reach):
    seq_index = lax.axis_index("zl") * lax.axis_size("core") + lax.axis_index("core")
    place = lax.broadcasted_iota(jnp.int32, (tok, tok), 0)
    query = lax.broadcasted_iota(jnp.int32, (tok, tok), 1)
    owner = seq_index + (part - 1)
    inside = jnp.logical_and(owner >= 0, owner < seq_devs)
    limit = jnp.where(inside, reach, -1)
    return jnp.abs(place - query + (part - 1) * tok) <= limit


def sort_halo(inside, outside, halo):
    core = lax.axis_index("core")

    @pl.when(core == 0)
    def _():
        halo[0] = outside[...]
        halo[1] = inside[...]

    @pl.when(core != 0)
    def _():
        halo[0] = inside[...]
        halo[1] = outside[...]


def head_probs(parts, query, reach, seq_devs):
    head, tok = query.shape
    scale = float(head) ** (-0.5)
    masks = [reached_part(p, tok, seq_devs, reach) for p in range(3)]
    scores = [
        jnp.where(masks[p], dot_first(parts[p][:head, :], query[...]) * scale, -1e30)
        for p in range(3)
    ]
    peak = functools.reduce(jnp.maximum, [jnp.max(s, axis=0, keepdims=True) for s in scores])
    weights = [jnp.where(masks[p], jnp.exp(scores[p] - peak), 0.0) for p in range(3)]
    total = sum(jnp.sum(w, axis=0, keepdims=True) for w in weights)
    inverse = 1.0 / total
    return [w * inverse for w in weights]


def own_reach(reaches):
    col_devs = lax.axis_size("zh") * lax.axis_size("x")
    col_index = lax.axis_index("zh") * lax.axis_size("x") + lax.axis_index("x")
    return reaches[lax.axis_index("row") * col_devs + col_index]


def attend_body(seq_devs, *refs):
    sources, (inside, outside, own), (send, hidden_ref) = refs[:5], refs[5:8], refs[8:10]
    query, stream, gain_row, reaches, halo, arrived = refs[10:]
    head, tok = query.shape
    cot_rows = send.at[head : 2 * head, :]
    load_all(sources, (query, stream, gain_row, reaches, cot_rows), arrived)
    sort_halo(inside, outside, halo)
    parts = (halo.at[0], own, halo.at[1])
    probs = head_probs(parts, query, own_reach(reaches), seq_devs)
    attended = sum(dot_plain(parts[p][head:, :], probs[p].astype(BF)) for p in range(3))
    hidden = (stream[...].astype(F32) + attended).astype(BF)
    hidden_ref[...] = hidden
    hidden_f = hidden.astype(F32)
    send[:head, :] = (hidden_f * column(gain_row[...])).astype(BF)
    write_tail(send, (), 2 * head, jnp.sum(hidden_f * hidden_f, axis=0, keepdims=True))


def project_body(head, slots, *refs):
    weights, (mine, theirs), (parts, feats, cots) = refs[:slots], refs[slots : slots + 2], refs[slots + 2 :]
    n_x, n_zh, _, tok = mine.shape
    units = weights[0].shape[2]
    blocks = weights[0].shape[0] // 2
    depth = n_x * n_zh * head
    core = lax.axis_index("core")

    def place(side, panel):
        lanes = slice(side * tok, (side + 1) * tok)
        for zh in range(n_zh):
            for x in range(n_x):
                rows = slice((zh * n_x + x) * head, (zh * n_x + x + 1) * head)
                feats[rows, lanes] = panel[x, zh, :head, :]
                cots[rows, lanes] = panel[x, zh, head : 2 * head, :]

    @pl.when(core == 0)
    def _():
        place(0, mine)
        place(1, theirs)

    @pl.when(core != 0)
    def _():
        place(0, theirs)
        place(1, mine)

    squares = [jnp.zeros((1, tok), F32), jnp.zeros((1, tok), F32)]
    for zh in range(n_zh):
        for x in range(n_x):
            for side, panel in enumerate((mine, theirs)):
                squares[side] += read_tail(panel[x, zh, 2 * head :, :])
    square = jnp.where(
        core == 0,
        jnp.concatenate(squares, axis=1),
        jnp.concatenate(squares[::-1], axis=1),
    )
    for w in range(slots):
        up = weights[w][:blocks].reshape(depth, units)
        parts[w, :units, :] = dot_first(up, feats[...]).astype(BF)
        total = jnp.zeros((units, 2 * tok), F32)
        for b in range(blocks):
            total += dot_plain(weights[w][blocks + b], cots[b * BLK : (b + 1) * BLK, :])
        parts[w, units : 2 * units, :] = total.astype(BF)
        write_tail(parts, (w,), 2 * units, square)


def norm_grad_body(head, n_zh, n_x, slots, acts, *refs):
    weights, out = refs[:slots], refs[slots]
    units = weights[0].shape[2]
    blocks = weights[0].shape[0] // 2
    tok = acts.shape[2] // 2
    per_block = BLK // head
    n_core = out.shape[0] // n_x
    for b in range(blocks):
        total = jnp.zeros((BLK, 2 * tok), F32)
        for w in range(slots):
            total += dot_plain(weights[w][b], acts[w, units : 2 * units, :])
        total = total.astype(BF)
        for k in range(per_block):
            zh, x = divmod(b * per_block + k, n_x)
            rows = slice(zh * head, (zh + 1) * head)
            for c in range(n_core):
                out[c * n_x + x, rows, :] = total[
                    k * head : (k + 1) * head, c * tok : (c + 1) * tok
                ]
    inner = sum(read_tail(acts[w, 2 * units :, :]) for w in range(slots))
    for x in range(n_x):
        for c in range(n_core):
            write_tail(out, (c * n_x + x,), n_zh * head, inner[:, c * tok : (c + 1) * tok])


def weight_grad_body(slots, acts, feats, cots, *homes):
    units = homes[0].shape[2]
    blocks = homes[0].shape[0] // 2
    for w in range(slots):
        grad = acts[w, units : 2 * units, :]
        homes[w][:blocks] = dot_last(feats[...], grad).astype(BF).reshape(blocks, BLK, units)
        active = acts[w, :units, :]
        for b in range(blocks):
            block = dot_last(active, cots[b * BLK : (b + 1) * BLK, :])
            homes[w][blocks + b] = block.astype(BF)


def x_sum_body(head, pieces, out):
    n_zh = out.shape[0]
    rows = n_zh * head
    inner = sum(read_tail(pieces[x, rows:, :]) for x in range(pieces.shape[0]))
    for zh in range(n_zh):
        span = slice(zh * head, (zh + 1) * head)
        total = sum(pieces[x, span, :].astype(F32) for x in range(pieces.shape[0]))
        out[zh, :head, :] = total.astype(BF)
        write_tail(out, (zh,), head, inner)


def probs_body(seq_devs, reaches, query, inside, outside, own, probs_ref, halo):
    sort_halo(inside, outside, halo)
    probs = head_probs((halo.at[0], own, halo.at[1]), query, own_reach(reaches), seq_devs)
    for p in range(3):
        probs_ref[p] = probs[p]


def attend_grad_body(width_total, *refs):
    cot, gain_row, probs, query, pieces, hidden, inv_rms, inside, outside, own = refs[:10]
    stream_out, query_out, inside_out, outside_out, own_out, gain_out, halo = refs[10:]
    head, tok = query.shape
    scale = float(head) ** (-0.5)
    grad_norm = sum(pieces[z, :head, :].astype(F32) for z in range(pieces.shape[0]))
    inner = sum(read_tail(pieces[z, head:, :]) for z in range(pieces.shape[0]))
    hidden_f = hidden[...].astype(F32)
    ones = jnp.ones((gain_out.shape[0], tok), F32)
    gain_out[...] = lax.dot_general(
        ones,
        grad_norm * hidden_f,
        (((1,), (1,)), ((), ())),
        precision=lax.Precision.HIGHEST,
        preferred_element_type=F32,
    )
    own_inv = jnp.where(lax.axis_index("core") == 0, inv_rms[:, :tok], inv_rms[:, tok:])
    shrink = own_inv * inner / width_total
    grad_hidden = column(gain_row[...]) * grad_norm - hidden_f * shrink + cot[...].astype(F32)
    grad_stream = grad_hidden.astype(BF)
    stream_out[...] = grad_stream
    sort_halo(inside, outside, halo)
    parts = (halo.at[0], own, halo.at[1])
    grad_probs = [dot_first(parts[p][head:, :], grad_stream) for p in range(3)]
    center = sum(jnp.sum(probs[p] * grad_probs[p], axis=0, keepdims=True) for p in range(3))
    grad_query = jnp.zeros((head, tok), F32)
    for p in range(3):
        grad_scores = (probs[p] * (grad_probs[p] - center)).astype(BF)
        grad_query += dot_plain(parts[p][:head, :], grad_scores)
        key_grad = dot_last(query[...], grad_scores) * scale
        value_grad = dot_last(grad_stream, probs[p].astype(BF))
        if p == 1:
            own_out[:head, :] = key_grad
            own_out[head:, :] = value_grad
        else:
            halo[p // 2, :head, :] = key_grad.astype(BF)
            halo[p // 2, head:, :] = value_grad.astype(BF)
    query_out[...] = (grad_query * scale).astype(BF)
    core = lax.axis_index("core")

    @pl.when(core == 0)
    def _():
        outside_out[...] = halo[0]
        inside_out[...] = halo[1]

    @pl.when(core != 0)
    def _():
        inside_out[...] = halo[0]
        outside_out[...] = halo[1]


def home_sum_body(slots, *refs):
    homes, (flags, grad_up, grad_down) = refs[:slots], refs[slots:]
    blocks = homes[0].shape[0] // 2
    for b in range(2 * blocks):
        total = sum(homes[w][b].astype(F32) for w in range(slots)) * flags[b : b + 1, :]
        if b < blocks:
            grad_up[b * BLK : (b + 1) * BLK, :] = total.astype(BF)
        else:
            grad_down[:, (b - blocks) * BLK : (b - blocks + 1) * BLK] = total.astype(BF)


def pair_sum_body(own, inside, outside, gains, key_out, value_out, gain_out):
    head = key_out.shape[0]
    gain_out[...] = jnp.sum(gains[...], axis=0, keepdims=True)
    total = (own[...] + inside[...].astype(F32) + outside[...].astype(F32)).astype(BF)
    key_out[...] = total[:head, :]
    value_out[...] = total[head:, :]


def on_device(
    stream,
    query_heads,
    key_heads,
    value_heads,
    windows,
    norm_gain,
    up_weight,
    down_weight,
    up_rows,
    up_cols,
    down_rows,
    down_cols,
    cotangent,
):
    tok, head = stream.shape
    n_zl, n_core, n_row, n_zh, n_x = (lax.axis_size(a) for a in ("zl", "core", "row", "zh", "x"))
    seq_devs = n_zl * n_core
    col_devs = n_zh * n_x
    row_index = lax.axis_index("row")
    col_index = lax.axis_index(("zh", "x"))
    width_total = head * n_row * col_devs
    depth, units = up_weight.shape
    blocks = depth // BLK
    both_toks = n_core * tok
    swap = [(i, n_core - 1 - i) for i in range(n_core)]
    cross = [(i, i + 1) for i in range(1, seq_devs - 1, 2)]
    cross += [(j, i) for i, j in cross]
    query_t, stream_t, cot_t = query_heads.T, stream.T, cotangent.T
    gain = norm_gain[None, :]

    ids = [a.reshape(-1, BLK) for a in (up_rows, up_cols, down_cols, down_rows)]
    both, flags, paired = call_kernel(
        functools.partial(prepare_body, blocks),
        [
            shaped((2 * blocks, BLK, units), BF),
            shaped((2 * blocks, BLK), F32),
            shaped((2 * head, tok), BF),
        ],
        0,
        up_weight,
        down_weight,
        *ids,
        key_heads.T,
        value_heads.T,
        loads=8,
        scratch=[held(a) for a in (up_weight, down_weight, *ids)],
    )
    inside = lax.ppermute(paired, "core", swap)
    outside = lax.ppermute(paired, ("zl", "core"), cross)

    halo = pltpu.VMEM((2, 2 * head, tok), BF)
    reaches = pltpu.SMEM(windows.shape, windows.dtype)
    send, hidden = call_kernel(
        functools.partial(attend_body, seq_devs),
        [shaped((2 * head + TAIL, tok), BF), shaped((head, tok), BF)],
        12 * tok * tok * head,
        query_t,
        stream_t,
        gain,
        windows,
        cot_t,
        inside,
        outside,
        paired,
        loads=5,
        scratch=[held(query_t), held(stream_t), held(gain), reaches, halo],
    )
    first = window_send(both, 1, n_zh, n_zl, n_core, False)

    panel = lax.all_gather(send, "zh", axis=0, tiled=False)
    panel, first, both = lax.optimization_barrier((panel, first, both))
    near = [
        window_send(first, 1, n_zh, n_zl, n_core, False),
        window_send(both, 3, n_zh, n_zl, n_core, False),
    ]
    panel = spread(panel, "x")
    panel, near = lax.optimization_barrier((panel, near))
    other = lax.ppermute(panel, "core", swap)
    slots = [near[0], first, both, near[1]]

    parts, feats, cots = call_kernel(
        functools.partial(project_body, head, n_zl),
        [
            shaped((n_zl, 2 * units + TAIL, both_toks), BF),
            shaped((depth, both_toks), BF),
            shaped((depth, both_toks), BF),
        ],
        4 * n_zl * depth * units * both_toks,
        *slots,
        panel,
        other,
    )
    parts = exchange(parts, "row")
    summed = jnp.sum(parts[:, : 2 * units].astype(F32), axis=0)
    square_total = jnp.sum(tail_value(parts[:, 2 * units :]), axis=0)
    inv_rms = lax.rsqrt(square_total / width_total + EPSILON)
    pre_act = summed[:units] * inv_rms
    activation = gelu_value(pre_act).astype(BF)
    grad_act = (summed[units:] * gelu_slope(pre_act) * inv_rms).astype(BF)
    inner_part = jnp.sum(grad_act.astype(F32) * pre_act, axis=0)
    acts = spread(jnp.concatenate([activation, grad_act, tail_rows(inner_part)], axis=0), "row")

    pieces = call_kernel(
        functools.partial(norm_grad_body, head, n_zh, n_x, n_zl),
        [shaped((n_core * n_x, n_zh * head + TAIL, tok), BF)],
        2 * n_zl * depth * units * both_toks,
        acts,
        *slots,
    )[0]
    homes = call_kernel(
        functools.partial(weight_grad_body, n_zl),
        [shaped((2 * blocks, BLK, units), BF)] * n_zl,
        4 * n_zl * depth * units * both_toks,
        acts,
        feats,
        cots,
    )
    pieces = exchange(pieces, ("core", "x"))
    pieces = call_kernel(
        functools.partial(x_sum_body, head),
        [shaped((n_zh, head + TAIL, tok), BF)],
        0,
        pieces,
    )[0]
    joined = window_send(homes[0], 1, n_zh, n_zl, n_core, True)
    early = window_send(homes[3], 3, n_zh, n_zl, n_core, True)
    query_t, feats = lax.optimization_barrier((query_t, feats))
    probs = call_kernel(
        functools.partial(probs_body, seq_devs),
        [shaped((3, tok, tok), F32)],
        4 * 10**9,
        windows,
        query_t,
        inside,
        outside,
        paired,
        scratch=[halo],
    )[0]
    pieces = exchange(pieces, "zh")
    joined = (homes[1].astype(F32) + joined.astype(F32)).astype(BF)
    late = window_send(joined, 1, n_zh, n_zl, n_core, True)
    pieces, early = lax.optimization_barrier((pieces, early))

    grad_stream, grad_query, inside_grad, outside_grad, own, gain_parts = call_kernel(
        functools.partial(attend_grad_body, width_total),
        [
            shaped((head, tok), BF),
            shaped((head, tok), BF),
            shaped((2 * head, tok), BF),
            shaped((2 * head, tok), BF),
            shaped((2 * head, tok), F32),
            shaped((seq_devs, head), F32),
        ],
        30 * tok * tok * head,
        cot_t,
        gain,
        probs,
        query_t,
        pieces,
        hidden,
        inv_rms[None],
        inside,
        outside,
        paired,
        scratch=[halo],
    )
    own, late = lax.optimization_barrier((own, late))
    gain_parts = exchange(gain_parts, ("zl", "core"))
    inside_grad = lax.ppermute(inside_grad, "core", swap)
    outside_grad = lax.ppermute(outside_grad, ("zl", "core"), cross)
    grad_up, grad_down = call_kernel(
        functools.partial(home_sum_body, 3),
        [shaped((depth, units), BF), shaped((units, depth), BF)],
        0,
        early,
        late,
        homes[2],
        flags,
    )
    grad_key, grad_value, grad_gain = call_kernel(
        pair_sum_body,
        [shaped((head, tok), BF), shaped((head, tok), BF), shaped((1, head), F32)],
        0,
        own,
        inside_grad,
        outside_grad,
        gain_parts,
    )
    grad_gain = grad_gain.reshape(head)
    return (
        grad_stream.T,
        grad_query.T,
        grad_key.T,
        grad_value.T,
        grad_gain,
        grad_up,
        grad_down,
    )


def solution(mesh):
    seq, row, col = (mesh.shape[a] for a in ("seq", "row", "col"))
    fine = Mesh(
        mesh.devices.reshape(seq // 2, 2, row, 4, col // 4), ("zl", "core", "row", "zh", "x")
    )
    features = P(("zl", "core"), ("row", "zh", "x"))
    gain_spec = P(("row", "zh", "x"))
    up_spec = P("row", ("zl", "core", "zh", "x"))
    down_spec = P(("zl", "core", "zh", "x"), "row")
    in_specs = (
        (features,) * 4 + (P(), gain_spec, up_spec, down_spec) + (P(),) * 4 + (features,)
    )
    out_specs = (features,) * 4 + (gain_spec, up_spec, down_spec)
    return jax.shard_map(
        on_device, mesh=fine, in_specs=in_specs, out_specs=out_specs, check_vma=False
    )
```

```python
import functools

import jax
import jax.numpy as jnp
from jax import lax
from jax.experimental import pallas as pl
from jax.experimental.pallas import tpu as pltpu
from jax.sharding import Mesh
from jax.sharding import PartitionSpec as P

BLK = 128
GELU_C = 0.7978845608028654
GELU_A = 0.044715
EPSILON = 1e-05
TAIL = 16
BF = jnp.bfloat16
F32 = jnp.float32


def gelu_value(pre_act):
    tanh_arg = GELU_C * (pre_act + GELU_A * pre_act * pre_act * pre_act)
    return 0.5 * pre_act * (1.0 + jnp.tanh(tanh_arg))


def gelu_slope(pre_act):
    tanh_arg = GELU_C * (pre_act + GELU_A * pre_act * pre_act * pre_act)
    tanh_val = jnp.tanh(tanh_arg)
    return 0.5 * (1.0 + tanh_val) + 0.5 * pre_act * (1.0 - tanh_val * tanh_val) * GELU_C * (
        1.0 + 3.0 * GELU_A * pre_act * pre_act
    )


def tail_rows(vector):
    high = lax.reduce_precision(vector, 8, 7)
    low = vector - high
    pair = jnp.stack([high, low]).astype(BF)
    return jnp.pad(pair, ((0, TAIL - 2), (0, 0)))


def tail_value(rows):
    return rows[..., 0, :].astype(F32) + rows[..., 1, :].astype(F32)


def spread(array, axis):
    count = lax.axis_size(axis)
    copies = jnp.broadcast_to(array[None], (count,) + array.shape)
    return lax.all_to_all(copies, axis, 0, 0, tiled=True)


def exchange(pieces, axis):
    return lax.all_to_all(pieces, axis, 0, 0, tiled=True)


def window_send(array, slot, n_zh, n_zl, n_core, home):
    ring = n_zh * n_zl
    pairs = []
    for place in range(ring):
        for core in range(n_core):
            step = (slot - n_zl // 2) * (1 if core == 0 else -1)
            owner, worker = (
                ((z % n_zl) * n_core + core) * n_zh + z // n_zl for z in ((place + step) % ring, place)
            )
            pairs.append((worker, owner) if home else (owner, worker))
    if all(source == target for source, target in pairs):
        return array
    return lax.ppermute(array, ("zl", "core", "zh"), pairs)


def call_kernel(body, out_shapes, flops, *operands, loads=0, scratch=()):
    moved = sum(a.size * a.dtype.itemsize for a in operands)
    moved += sum(a.size * a.dtype.itemsize for a in out_shapes)
    vmem = pl.BlockSpec(memory_space=pltpu.VMEM)
    smem = pl.BlockSpec(memory_space=pltpu.SMEM)
    return pl.pallas_call(
        body,
        out_shape=out_shapes,
        in_specs=[pl.BlockSpec(memory_space=pltpu.HBM)] * loads
        + [smem if a.ndim == 1 else vmem for a in operands[loads:]],
        out_specs=[vmem] * len(out_shapes),
        scratch_shapes=list(scratch) + ([pltpu.SemaphoreType.DMA((loads,))] if loads else []),
        compiler_params=pltpu.CompilerParams(vmem_limit_bytes=(60 if loads else 24) * 1024 * 1024),
        cost_estimate=pl.CostEstimate(flops=flops, bytes_accessed=moved, transcendentals=0),
    )(*operands)


def load_all(sources, targets, arrived):
    copies = [
        pltpu.make_async_copy(source, target, arrived.at[i])
        for i, (source, target) in enumerate(zip(sources, targets, strict=True))
    ]
    for copy in copies:
        copy.start()
    for copy in copies:
        copy.wait()


def held(array):
    return pltpu.VMEM(array.shape, array.dtype)


def shaped(shape, dtype):
    return jax.ShapeDtypeStruct(shape, dtype)


def dot_first(left, right):
    return lax.dot_general(left, right, (((0,), (0,)), ((), ())), preferred_element_type=F32)


def dot_last(left, right):
    return lax.dot_general(left, right, (((1,), (1,)), ((), ())), preferred_element_type=F32)


def dot_plain(left, right):
    return jnp.dot(left, right, preferred_element_type=F32)


def write_tail(ref, index, first, vector):
    high = vector.astype(BF)
    low = (vector - high.astype(F32)).astype(BF)
    place = lax.broadcasted_iota(jnp.int32, (TAIL, vector.shape[1]), 0)
    rows = jnp.where(place == 0, high.astype(F32), jnp.where(place == 1, low.astype(F32), 0.0))
    ref[index + (slice(first, first + TAIL), slice(None))] = rows.astype(BF)


def read_tail(rows):
    rows = rows.astype(F32)
    return rows[0:1] + rows[1:2]


def prepare_body(blocks, *refs):
    sources, (both_ref, flag_ref, pair_ref) = refs[:8], refs[8:11]
    up_ref, down_ref, up_in, up_out, down_in, down_out, arrived = refs[11:]
    head = sources[6].shape[0]
    pair_halves = (pair_ref.at[:head, :], pair_ref.at[head:, :])
    load_all(sources, (up_ref, down_ref, up_in, up_out, down_in, down_out) + pair_halves, arrived)
    col_devs = lax.axis_size("zh") * lax.axis_size("x")
    seq_index = lax.axis_index("zl") * lax.axis_size("core") + lax.axis_index("core")
    col_index = lax.axis_index("zh") * lax.axis_size("x") + lax.axis_index("x")
    own_block = seq_index * col_devs + col_index
    first = lax.axis_index("row") * blocks
    for kind, (inner, outer) in enumerate(((up_in, up_out), (down_in, down_out))):
        shifted = jnp.where(outer[...] == own_block, inner[...] - first, -1)
        for b in range(blocks):
            hit = jnp.where(shifted == b, 1.0, 0.0)
            flag = jnp.max(jnp.max(hit, axis=0, keepdims=True), axis=1, keepdims=True)
            flag_ref[kind * blocks + b : kind * blocks + b + 1, :] = jnp.broadcast_to(flag, (1, BLK))
            if kind == 0:
                block = up_ref[b * BLK : (b + 1) * BLK, :]
            else:
                block = down_ref[:, b * BLK : (b + 1) * BLK]
            both_ref[kind * blocks + b] = (block.astype(F32) * flag).astype(BF)


def column(row):
    count = row.shape[1]
    across = lax.broadcasted_iota(jnp.int32, (count, count), 1)
    down = lax.broadcasted_iota(jnp.int32, (count, count), 0)
    return jnp.sum(jnp.where(across == down, row, 0.0), axis=1, keepdims=True)


def reached_part(part, tok, seq_devs, reach):
    seq_index = lax.axis_index("zl") * lax.axis_size("core") + lax.axis_index("core")
    place = lax.broadcasted_iota(jnp.int32, (tok, tok), 0)
    query = lax.broadcasted_iota(jnp.int32, (tok, tok), 1)
    owner = seq_index + (part - 1)
    inside = jnp.logical_and(owner >= 0, owner < seq_devs)
    limit = jnp.where(inside, reach, -1)
    return jnp.abs(place - query + (part - 1) * tok) <= limit


def sort_halo(inside, outside, halo):
    core = lax.axis_index("core")

    @pl.when(core == 0)
    def _():
        halo[0] = outside[...]
        halo[1] = inside[...]

    @pl.when(core != 0)
    def _():
        halo[0] = inside[...]
        halo[1] = outside[...]


def head_probs(parts, query, reach, seq_devs):
    head, tok = query.shape
    scale = float(head) ** (-0.5)
    masks = [reached_part(p, tok, seq_devs, reach) for p in range(3)]
    scores = [
        jnp.where(masks[p], dot_first(parts[p][:head, :], query[...]) * scale, -1e30)
        for p in range(3)
    ]
    peak = functools.reduce(jnp.maximum, [jnp.max(s, axis=0, keepdims=True) for s in scores])
    weights = [jnp.where(masks[p], jnp.exp(scores[p] - peak), 0.0) for p in range(3)]
    total = sum(jnp.sum(w, axis=0, keepdims=True) for w in weights)
    inverse = 1.0 / total
    return [w * inverse for w in weights]


def own_reach(reaches):
    col_devs = lax.axis_size("zh") * lax.axis_size("x")
    col_index = lax.axis_index("zh") * lax.axis_size("x") + lax.axis_index("x")
    return reaches[lax.axis_index("row") * col_devs + col_index]


def attend_body(seq_devs, *refs):
    sources, (send, hidden_ref) = refs[:8], refs[8:10]
    query, stream, gain_row, reaches, own, halo, arrived = refs[10:]
    head, tok = query.shape
    cot_rows = send.at[head : 2 * head, :]
    core = lax.axis_index("core")
    sides = (halo.at[1 - core], halo.at[core])
    load_all(sources, (query, stream, gain_row, reaches, cot_rows, own) + sides, arrived)
    parts = (halo.at[0], own, halo.at[1])
    probs = head_probs(parts, query, own_reach(reaches), seq_devs)
    attended = sum(dot_plain(parts[p][head:, :], probs[p].astype(BF)) for p in range(3))
    hidden = (stream[...].astype(F32) + attended).astype(BF)
    hidden_ref[...] = hidden
    hidden_f = hidden.astype(F32)
    send[:head, :] = (hidden_f * column(gain_row[...])).astype(BF)
    write_tail(send, (), 2 * head, jnp.sum(hidden_f * hidden_f, axis=0, keepdims=True))


def project_body(head, slots, *refs):
    weights, (mine, theirs), (parts, feats, cots) = refs[:slots], refs[slots : slots + 2], refs[slots + 2 :]
    n_x, n_zh, _, tok = mine.shape
    units = weights[0].shape[2]
    blocks = weights[0].shape[0] // 2
    depth = n_x * n_zh * head
    core = lax.axis_index("core")

    def place(side, panel):
        lanes = slice(side * tok, (side + 1) * tok)
        for zh in range(n_zh):
            for x in range(n_x):
                rows = slice((zh * n_x + x) * head, (zh * n_x + x + 1) * head)
                feats[rows, lanes] = panel[x, zh, :head, :]
                cots[rows, lanes] = panel[x, zh, head : 2 * head, :]

    @pl.when(core == 0)
    def _():
        place(0, mine)
        place(1, theirs)

    @pl.when(core != 0)
    def _():
        place(0, theirs)
        place(1, mine)

    squares = [jnp.zeros((1, tok), F32), jnp.zeros((1, tok), F32)]
    for zh in range(n_zh):
        for x in range(n_x):
            for side, panel in enumerate((mine, theirs)):
                squares[side] += read_tail(panel[x, zh, 2 * head :, :])
    square = jnp.where(
        core == 0,
        jnp.concatenate(squares, axis=1),
        jnp.concatenate(squares[::-1], axis=1),
    )
    for w in range(slots):
        up = weights[w][:blocks].reshape(depth, units)
        parts[w, :units, :] = dot_first(up, feats[...]).astype(BF)
        total = jnp.zeros((units, 2 * tok), F32)
        for b in range(blocks):
            total += dot_plain(weights[w][blocks + b], cots[b * BLK : (b + 1) * BLK, :])
        parts[w, units : 2 * units, :] = total.astype(BF)
        write_tail(parts, (w,), 2 * units, square)


def norm_grad_body(head, n_zh, n_x, slots, acts, *refs):
    weights, outs = refs[:slots], refs[slots:]
    units = weights[0].shape[2]
    blocks = weights[0].shape[0] // 2
    tok = acts.shape[2] // 2
    per_block = BLK // head
    core = lax.axis_index("core")
    for b in range(blocks):
        total = jnp.zeros((BLK, 2 * tok), F32)
        for w in range(slots):
            total += dot_plain(weights[w][b], acts[w, units : 2 * units, :])
        first, second = total[:, :tok], total[:, tok:]
        halves = (jnp.where(core == 0, first, second), jnp.where(core == 0, second, first))
        for half, out in zip(halves, outs, strict=True):
            half = half.astype(BF)
            for k in range(per_block):
                zh, x = divmod(b * per_block + k, n_x)
                rows = slice(zh * head, (zh + 1) * head)
                out[x, rows, :] = half[k * head : (k + 1) * head, :]
    inner = sum(read_tail(acts[w, 2 * units :, :]) for w in range(slots))
    first, second = inner[:, :tok], inner[:, tok:]
    halves = (jnp.where(core == 0, first, second), jnp.where(core == 0, second, first))
    for half, out in zip(halves, outs, strict=True):
        for x in range(n_x):
            write_tail(out, (x,), n_zh * head, half)


def weight_grad_body(slots, acts, feats, cots, *homes):
    units = homes[0].shape[2]
    blocks = homes[0].shape[0] // 2
    for w in range(slots):
        grad = acts[w, units : 2 * units, :]
        homes[w][:blocks] = dot_last(feats[...], grad).astype(BF).reshape(blocks, BLK, units)
        active = acts[w, :units, :]
        for b in range(blocks):
            block = dot_last(active, cots[b * BLK : (b + 1) * BLK, :])
            homes[w][blocks + b] = block.astype(BF)


def core_sum_body(rows, own, theirs, out):
    for x in range(own.shape[0]):
        total = own[x, :rows, :].astype(F32) + theirs[x, :rows, :].astype(F32)
        out[x, :rows, :] = total.astype(BF)
        write_tail(out, (x,), rows, read_tail(own[x, rows:, :]) + read_tail(theirs[x, rows:, :]))


def x_sum_body(head, pieces, out):
    n_zh = out.shape[0]
    rows = n_zh * head
    inner = sum(read_tail(pieces[x, rows:, :]) for x in range(pieces.shape[0]))
    for zh in range(n_zh):
        span = slice(zh * head, (zh + 1) * head)
        total = sum(pieces[x, span, :].astype(F32) for x in range(pieces.shape[0]))
        out[zh, :head, :] = total.astype(BF)
        write_tail(out, (zh,), head, inner)


def probs_body(seq_devs, reaches, query, inside, outside, own, probs_ref, halo):
    sort_halo(inside, outside, halo)
    probs = head_probs((halo.at[0], own, halo.at[1]), query, own_reach(reaches), seq_devs)
    for p in range(3):
        probs_ref[p] = probs[p]


def attend_grad_body(width_total, *refs):
    cot, gain_row, probs, query, pieces, hidden, inv_rms, inside, outside, own = refs[:10]
    stream_out, query_out, inside_out, outside_out, own_out, gain_out, halo = refs[10:]
    head, tok = query.shape
    scale = float(head) ** (-0.5)
    grad_norm = sum(pieces[z, :head, :].astype(F32) for z in range(pieces.shape[0]))
    inner = sum(read_tail(pieces[z, head:, :]) for z in range(pieces.shape[0]))
    hidden_f = hidden[...].astype(F32)
    ones = jnp.ones((gain_out.shape[0], tok), F32)
    gain_out[...] = lax.dot_general(
        ones,
        grad_norm * hidden_f,
        (((1,), (1,)), ((), ())),
        precision=lax.Precision.HIGHEST,
        preferred_element_type=F32,
    )
    own_inv = jnp.where(lax.axis_index("core") == 0, inv_rms[:, :tok], inv_rms[:, tok:])
    shrink = own_inv * inner / width_total
    grad_hidden = column(gain_row[...]) * grad_norm - hidden_f * shrink + cot[...].astype(F32)
    grad_stream = grad_hidden.astype(BF)
    stream_out[...] = grad_stream
    sort_halo(inside, outside, halo)
    parts = (halo.at[0], own, halo.at[1])
    grad_probs = [dot_first(parts[p][head:, :], grad_stream) for p in range(3)]
    center = sum(jnp.sum(probs[p] * grad_probs[p], axis=0, keepdims=True) for p in range(3))
    grad_query = jnp.zeros((head, tok), F32)
    for p in range(3):
        grad_scores = (probs[p] * (grad_probs[p] - center)).astype(BF)
        grad_query += dot_plain(parts[p][:head, :], grad_scores)
        key_grad = dot_last(query[...], grad_scores) * scale
        value_grad = dot_last(grad_stream, probs[p].astype(BF))
        if p == 1:
            own_out[:head, :] = key_grad
            own_out[head:, :] = value_grad
        else:
            halo[p // 2, :head, :] = key_grad.astype(BF)
            halo[p // 2, head:, :] = value_grad.astype(BF)
    query_out[...] = (grad_query * scale).astype(BF)
    core = lax.axis_index("core")

    @pl.when(core == 0)
    def _():
        outside_out[...] = halo[0]
        inside_out[...] = halo[1]

    @pl.when(core != 0)
    def _():
        inside_out[...] = halo[0]
        outside_out[...] = halo[1]


def home_sum_body(slots, *refs):
    homes, (flags, grad_up, grad_down) = refs[:slots], refs[slots:]
    blocks = homes[0].shape[0] // 2
    for b in range(2 * blocks):
        total = sum(homes[w][b].astype(F32) for w in range(slots)) * flags[b : b + 1, :]
        if b < blocks:
            grad_up[b * BLK : (b + 1) * BLK, :] = total.astype(BF)
        else:
            grad_down[:, (b - blocks) * BLK : (b - blocks + 1) * BLK] = total.astype(BF)


def pair_sum_body(own, inside, outside, gains, key_out, value_out, gain_out):
    head = key_out.shape[0]
    gain_out[...] = jnp.sum(gains[...], axis=0, keepdims=True)
    total = (own[...] + inside[...].astype(F32) + outside[...].astype(F32)).astype(BF)
    key_out[...] = total[:head, :]
    value_out[...] = total[head:, :]


def on_device(
    stream,
    query_heads,
    key_heads,
    value_heads,
    windows,
    norm_gain,
    up_weight,
    down_weight,
    up_rows,
    up_cols,
    down_rows,
    down_cols,
    cotangent,
):
    tok, head = stream.shape
    n_zl, n_core, n_row, n_zh, n_x = (lax.axis_size(a) for a in ("zl", "core", "row", "zh", "x"))
    seq_devs = n_zl * n_core
    col_devs = n_zh * n_x
    row_index = lax.axis_index("row")
    col_index = lax.axis_index(("zh", "x"))
    width_total = head * n_row * col_devs
    depth, units = up_weight.shape
    blocks = depth // BLK
    both_toks = n_core * tok
    swap = [(i, n_core - 1 - i) for i in range(n_core)]
    cross = [(i, i + 1) for i in range(1, seq_devs - 1, 2)]
    cross += [(j, i) for i, j in cross]
    query_t, stream_t, cot_t = query_heads.T, stream.T, cotangent.T
    gain = norm_gain[None, :]

    ids = [a.reshape(-1, BLK) for a in (up_rows, up_cols, down_cols, down_rows)]
    both, flags, paired = call_kernel(
        functools.partial(prepare_body, blocks),
        [
            shaped((2 * blocks, BLK, units), BF),
            shaped((2 * blocks, BLK), F32),
            shaped((2 * head, tok), BF),
        ],
        0,
        up_weight,
        down_weight,
        *ids,
        key_heads.T,
        value_heads.T,
        loads=8,
        scratch=[held(a) for a in (up_weight, down_weight, *ids)],
    )
    inside = lax.ppermute(paired, "core", swap)
    outside = lax.ppermute(paired, ("zl", "core"), cross)

    halo = pltpu.VMEM((2, 2 * head, tok), BF)
    reaches = pltpu.SMEM(windows.shape, windows.dtype)
    send, hidden = call_kernel(
        functools.partial(attend_body, seq_devs),
        [shaped((2 * head + TAIL, tok), BF), shaped((head, tok), BF)],
        12 * tok * tok * head,
        query_t,
        stream_t,
        gain,
        windows,
        cot_t,
        paired,
        inside,
        outside,
        loads=8,
        scratch=[held(query_t), held(stream_t), held(gain), reaches, held(paired), halo],
    )
    first = window_send(both, 1, n_zh, n_zl, n_core, False)

    panel = lax.all_gather(send, "zh", axis=0, tiled=False)
    panel, first, both = lax.optimization_barrier((panel, first, both))
    near = [
        window_send(first, 1, n_zh, n_zl, n_core, False),
        window_send(both, 3, n_zh, n_zl, n_core, False),
    ]
    panel = spread(panel, "x")
    panel, near = lax.optimization_barrier((panel, near))
    other = lax.ppermute(panel, "core", swap)
    slots = [near[0], first, both, near[1]]

    parts, feats, cots = call_kernel(
        functools.partial(project_body, head, n_zl),
        [
            shaped((n_zl, 2 * units + TAIL, both_toks), BF),
            shaped((depth, both_toks), BF),
            shaped((depth, both_toks), BF),
        ],
        4 * n_zl * depth * units * both_toks,
        *slots,
        panel,
        other,
    )
    parts = exchange(parts, "row")
    summed = jnp.sum(parts[:, : 2 * units].astype(F32), axis=0)
    square_total = jnp.sum(tail_value(parts[:, 2 * units :]), axis=0)
    inv_rms = lax.rsqrt(square_total / width_total + EPSILON)
    pre_act = summed[:units] * inv_rms
    activation = gelu_value(pre_act).astype(BF)
    grad_act = (summed[units:] * gelu_slope(pre_act) * inv_rms).astype(BF)
    inner_part = jnp.sum(grad_act.astype(F32) * pre_act, axis=0)
    acts = spread(jnp.concatenate([activation, grad_act, tail_rows(inner_part)], axis=0), "row")

    mine, theirs = call_kernel(
        functools.partial(norm_grad_body, head, n_zh, n_x, n_zl),
        [shaped((n_x, n_zh * head + TAIL, tok), BF)] * 2,
        2 * n_zl * depth * units * both_toks,
        acts,
        *slots,
    )
    theirs = lax.ppermute(theirs, "core", swap)
    homes = call_kernel(
        functools.partial(weight_grad_body, n_zl),
        [shaped((2 * blocks, BLK, units), BF)] * n_zl,
        4 * n_zl * depth * units * both_toks,
        acts,
        feats,
        cots,
    )
    pieces = call_kernel(
        functools.partial(core_sum_body, n_zh * head),
        [shaped((n_x, n_zh * head + TAIL, tok), BF)],
        0,
        mine,
        theirs,
    )[0]
    pieces = exchange(pieces, "x")
    pieces = call_kernel(
        functools.partial(x_sum_body, head),
        [shaped((n_zh, head + TAIL, tok), BF)],
        0,
        pieces,
    )[0]
    joined = window_send(homes[0], 1, n_zh, n_zl, n_core, True)
    early = window_send(homes[3], 3, n_zh, n_zl, n_core, True)
    query_t, feats = lax.optimization_barrier((query_t, feats))
    probs = call_kernel(
        functools.partial(probs_body, seq_devs),
        [shaped((3, tok, tok), F32)],
        4 * 10**9,
        windows,
        query_t,
        inside,
        outside,
        paired,
        scratch=[halo],
    )[0]
    pieces = exchange(pieces, "zh")
    joined = (homes[1].astype(F32) + joined.astype(F32)).astype(BF)
    late = window_send(joined, 1, n_zh, n_zl, n_core, True)
    pieces, early = lax.optimization_barrier((pieces, early))

    grad_stream, grad_query, inside_grad, outside_grad, own, gain_parts = call_kernel(
        functools.partial(attend_grad_body, width_total),
        [
            shaped((head, tok), BF),
            shaped((head, tok), BF),
            shaped((2 * head, tok), BF),
            shaped((2 * head, tok), BF),
            shaped((2 * head, tok), F32),
            shaped((seq_devs, head), F32),
        ],
        30 * tok * tok * head,
        cot_t,
        gain,
        probs,
        query_t,
        pieces,
        hidden,
        inv_rms[None],
        inside,
        outside,
        paired,
        scratch=[halo],
    )
    own, late = lax.optimization_barrier((own, late))
    gain_parts = exchange(gain_parts, ("zl", "core"))
    inside_grad = lax.ppermute(inside_grad, "core", swap)
    outside_grad = lax.ppermute(outside_grad, ("zl", "core"), cross)
    grad_up, grad_down = call_kernel(
        functools.partial(home_sum_body, 3),
        [shaped((depth, units), BF), shaped((units, depth), BF)],
        0,
        early,
        late,
        homes[2],
        flags,
    )
    grad_key, grad_value, grad_gain = call_kernel(
        pair_sum_body,
        [shaped((head, tok), BF), shaped((head, tok), BF), shaped((1, head), F32)],
        0,
        own,
        inside_grad,
        outside_grad,
        gain_parts,
    )
    grad_gain = grad_gain.reshape(head)
    return (
        grad_stream.T,
        grad_query.T,
        grad_key.T,
        grad_value.T,
        grad_gain,
        grad_up,
        grad_down,
    )


def solution(mesh):
    seq, row, col = (mesh.shape[a] for a in ("seq", "row", "col"))
    fine = Mesh(
        mesh.devices.reshape(seq // 2, 2, row, 4, col // 4), ("zl", "core", "row", "zh", "x")
    )
    features = P(("zl", "core"), ("row", "zh", "x"))
    gain_spec = P(("row", "zh", "x"))
    up_spec = P("row", ("zl", "core", "zh", "x"))
    down_spec = P(("zl", "core", "zh", "x"), "row")
    in_specs = (
        (features,) * 4 + (P(), gain_spec, up_spec, down_spec) + (P(),) * 4 + (features,)
    )
    out_specs = (features,) * 4 + (gain_spec, up_spec, down_spec)
    return jax.shard_map(
        on_device, mesh=fine, in_specs=in_specs, out_specs=out_specs, check_vma=False
    )
```
